32 devices in a mesh: gx: 8 (over z, y), gy: 4 (over x, core).
Axes of the slice: x: 2, y: 2, z: 4, core: 2. Of those that a mesh axis runs over, the one named last changes fastest.
Arguments:
- stored_slab: bfloat16 [2, 32, 64, 512], P(None, None, 'gx', 'gy'), may hold values from -6 to 6
- block_scales: bfloat16 [2, 32, 8, 4], P(None, None, 'gx', 'gy'), may hold values from 0.5 to 2
- holder: int32 [4], replicated, may hold values from 0 to 3, each once
- soil_class: int32 [64, 512], P('gx', 'gy'), may hold values from 0 to 11
- soil_table: float32 [12, 4], replicated, may hold values from 0.01 to 0.05
- cotangent: float32 [2, 32, 64, 512], P(None, None, 'gx', 'gy'), may hold values from -6 to 6
Outputs:
- recomputed: float32 [2, 32, 64, 512], P(None, None, 'gx', 'gy')
- sensitivity: float32 [2, 32, 64, 512], P(None, None, 'gx', 'gy')
The draws below stay inside these ranges and needn't reach their ends.
Inputs may be any that keep to these rules, and one draw needn't show every extreme that they name: holder is a permutation: every gy index holds exactly one checkpoint block.
All inputs are finite; a program needn't handle non-finite values.
Results may differ from the reference program's by a relative error of at most 0.0003.
Values may be sent and summed in bfloat16 or wider, within the bound.
A program may use at most 128 MiB of HBM per device.

```python
import math
import jax
import jax.numpy as jnp
from jax import lax

CX = 8
CY = 128
NZ = 32
NCLASS = 12
NX = 64
NY = 512
N_GX = 8
N_GY = 4


def set_ends(entries, rng, smallest, high):
    spot = [jax.random.randint(jax.random.fold_in(rng, axis), (), 0, length) for axis, length in enumerate(entries.shape)]
    longest = entries.shape.index(max(entries.shape))
    beside = spot[:longest] + [(spot[longest] + 1) % entries.shape[longest]] + spot[longest + 1:]
    return entries.at[tuple(spot)].set(smallest).at[tuple(beside)].set(high)


def level_of(own_key, shape, shards, least, high):
    def one(position, blocks):
        heights = jax.random.uniform(jax.random.fold_in(jax.random.fold_in(own_key, 6), position), (blocks,), jnp.float32, least / len(shards), high / len(shards))
        return jnp.repeat(jnp.exp(heights), shape[position] // blocks).reshape((-1,) + (1,) * (len(shape) - position - 1))

    loudness = one(*shards[0])
    for cut in shards[1:]:
        loudness = loudness * one(*cut)
    return loudness


def scatter_about(own_key, shape, width, reach, pieces=(), kind=jnp.bfloat16):
    entries = jax.random.normal(own_key, shape, jnp.float32) * width
    if len(pieces) > 0:
        entries = level_of(own_key, shape, pieces, -0.22, 0.18) * entries
    return jnp.clip(entries, min=-reach, max=reach).astype(kind)


def setup_inputs(seed: int = 0) -> dict:
    keys = jax.random.split(jax.random.key(seed), 7)
    return {
        "stored_slab": scatter_about(keys[0], (2, NZ, NX, NY), 1.0, 6.0, ((2, 8), (3, 4))),
        "block_scales": jnp.clip(jnp.exp(math.log(2.0) - 1.3862944 * jax.random.uniform(keys[1], (2, NZ, N_GX, N_GY), jnp.float32) ** level_of(keys[1], (2, NZ, N_GX, N_GY), ((2, 8), (3, 4)), -0.2, 0.2)), 0.5, 2.0).astype(jnp.bfloat16),
        "holder": jax.random.permutation(keys[2], N_GY).astype(jnp.int32),
        "soil_class": set_ends(jax.random.randint(keys[3], (NX, NY), 0, NCLASS), jax.random.fold_in(keys[3], 1), 0, NCLASS - 1).astype(jnp.int32),
        "soil_table": jnp.clip(jnp.exp(jax.random.uniform(keys[4], (NCLASS, 4), jnp.float32, math.log(0.01), math.log(0.05))), 0.01, 0.05),
        "cotangent": scatter_about(keys[5], (2, NZ, NX, NY), 1.0, 6.0, ((2, 8), (3, 4)), jnp.float32),
    }


OFFSETS = ((1, 0, 0), (-1, 0, 0), (0, 1, 0), (0, -1, 0), (0, 0, 1), (0, 0, -1))

def shifted(block, offset):
    sz, sx, sy = block.shape
    return block[1 + offset[0]:sz - 1 + offset[0], 1 + offset[1]:sx - 1 + offset[1], 1 + offset[2]:sy - 1 + offset[2]]

def spread(field, conduct):
    padded = jnp.pad(field, ((1, 1), (0, 0), (0, 0)))
    cond_pad = jnp.pad(conduct, ((1, 1), (0, 0), (0, 0)))
    middle = shifted(padded, (0, 0, 0))
    mid_cond = shifted(cond_pad, (0, 0, 0))
    summed = jnp.zeros_like(middle)
    for offset in OFFSETS:
        beside = shifted(padded, offset)
        near_cond = shifted(cond_pad, offset)
        summed = summed + 0.5 * (mid_cond + near_cond) * (beside - middle)
    return summed

def tendency(state, coefs):
    suction = state[0]
    warmth = state[1]
    bending = jnp.tanh(suction)
    strong = 1.5 + bending
    gentle = 1.5 + 0.5 * bending
    water_flow = spread(suction, coefs[0] * strong) + spread(warmth, coefs[1] * gentle)
    energy = spread(warmth, coefs[2] * gentle) + spread(suction, coefs[3] * strong)
    return jnp.stack([water_flow, energy])

def forward_all(state, coefs):
    padded = jnp.pad(state, ((0, 0), (0, 0), (1, 1), (1, 1)))
    cond_pad = jnp.pad(coefs, ((0, 0), (0, 0), (1, 1), (1, 1)))

    def block_step(index):
        start = index * CX
        piece = lax.dynamic_slice_in_dim(padded, start, CX + 2, 2)
        cond_piece = lax.dynamic_slice_in_dim(cond_pad, start, CX + 2, 2)
        return tendency(piece, cond_piece)
    blocks = lax.map(block_step, jnp.arange(N_GX, dtype=jnp.int32))
    return jnp.moveaxis(blocks, 0, 2).reshape(2, NZ, NX, NY)

def adjoint_all(state, coefs, adjoint):
    padded = jnp.pad(state, ((0, 0), (0, 0), (2, 2), (2, 2)))
    cond_pad = jnp.pad(coefs, ((0, 0), (0, 0), (2, 2), (2, 2)))
    adj_pad = jnp.pad(adjoint, ((0, 0), (0, 0), (1, 1), (1, 1)))

    def block_step(index):
        start = index * CX
        piece = lax.dynamic_slice_in_dim(padded, start, CX + 4, 2)
        cond_piece = lax.dynamic_slice_in_dim(cond_pad, start, CX + 4, 2)
        adj_piece = lax.dynamic_slice_in_dim(adj_pad, start, CX + 2, 2)

        def tendency_at(field):
            return tendency(field, cond_piece)
        _, pullback = jax.vjp(tendency_at, piece)
        pulled = pullback(adj_piece)[0]
        return pulled[:, :, 2:-2, 2:-2]
    blocks = lax.map(block_step, jnp.arange(N_GX, dtype=jnp.int32))
    return jnp.moveaxis(blocks, 0, 2).reshape(2, NZ, NX, NY)

def reference(stored_slab, block_scales, holder, soil_class, soil_table, cotangent):
    slab = stored_slab.astype(jnp.float32).reshape(2, NZ, NX, N_GY, CY)
    slab = jnp.take(slab, holder, axis=3)
    scales = jnp.take(block_scales.astype(jnp.float32), holder, axis=3)
    state0 = (slab.reshape(2, NZ, N_GX, CX, N_GY, CY) * scales[:, :, :, None, :, None]).reshape(2, NZ, NX, NY)
    coefs = jnp.transpose(soil_table[soil_class], (2, 0, 1))[:, None]
    state1 = state0 + forward_all(state0, coefs)
    state2 = state1 + forward_all(state1, coefs)
    adjoint1 = cotangent + adjoint_all(state1, coefs, cotangent)
    adjoint0 = adjoint1 + adjoint_all(state0, coefs, adjoint1)
    return (state2, adjoint0)
```

```python
import functools

import jax
import jax.numpy as jnp
from jax import lax
from jax.experimental import pallas as pl
from jax.experimental.pallas import tpu as pltpu
from jax.sharding import PartitionSpec as P

MESH = pl.DeviceIdType.MESH
COT, ST0, ST1, ADJ = range(4)


def window(
    n_gx, n_gy, nz, holder, table, slab, scale, classes, cot, out2, outs,
    slots, sslots, m0, m1, g0, g1, left0, right0, xs, xr, sx, ys, yr, sy, coef,
    gsend, grecv, lsem, xsend, xrecv, ysend, yrecv,
):
    gx, gy = lax.axis_index("gx"), lax.axis_index("gy")
    cx, cy = classes.shape
    half = n_gy // 2
    partner = gy + 1 - 2 * lax.rem(gy, 2)
    lane = lax.broadcasted_iota(jnp.int32, (cx, cy), 1)
    sub = lax.broadcasted_iota(jnp.int32, (cx, cy), 0)
    first_row, last_row = sub == 0, sub == cx - 1
    first_lane, last_lane = lane == 0, lane == cy - 1
    x_has = (gx > 0, gx < n_gx - 1)
    y_has = (gy > 0, gy < n_gy - 1)

    barrier = pltpu.get_barrier_semaphore()
    for k in range(1, n_gy):
        pl.semaphore_signal(barrier, inc=1, device_id=(gx, lax.rem(gy + k, n_gy)), device_id_type=MESH)
    for side, there in ((0, gx - 1), (1, gx + 1)):
        @pl.when(x_has[side])
        def _():
            pl.semaphore_signal(barrier, inc=1, device_id=(there, gy), device_id_type=MESH)

    own = [
        pltpu.make_async_copy(slab, slots.at[gy], lsem.at[0]),
        pltpu.make_async_copy(scale, sslots.at[gy], lsem.at[1]),
    ]
    for copy in own:
        copy.start()

    for side in range(2):
        @pl.when(jnp.logical_not(x_has[side]))
        def _():
            for e in range(4):
                xr[e, side] = jnp.zeros(xr.shape[2:], jnp.float32)

        @pl.when(jnp.logical_not(y_has[side]))
        def _():
            for e in range(3):
                yr[e, side] = jnp.zeros((cx, cy), jnp.float32)

    for ref in (m0, m1, g0, g1):
        for q in range(ref.shape[0]):
            ref[q, 0] = jnp.zeros((cx, cy), jnp.float32)
            ref[q, nz + 1] = jnp.zeros((cx, cy), jnp.float32)

    def to_lane(value, lane_from, lane_to):
        return pltpu.roll(value, lax.rem(lane_to - lane_from + cy, cy), 1)

    def edges_x(e, row, value):
        xs[e, 0, row] = value[0:1]
        xs[e, 1, row] = value[cx - 1 : cx]

    def edges_y(carry, slot, value):
        low, high = carry
        here = lane == slot
        return (
            jnp.where(here, to_lane(value, 0, slot), low),
            jnp.where(here, to_lane(value, cy - 1, slot), high),
        )

    blank = (jnp.zeros((cx, cy), jnp.float32),) * 2

    kind = classes[...]
    for k in range(4):
        value = jnp.zeros((cx, cy), jnp.float32)
        for c in range(table.shape[0]):
            value = jnp.where(kind == c, table[c, k], value)
        coef[0, k] = value
        edges_x(COT, 2 * nz + k, value)

    def cot_layer(z, carry):
        for f in range(2):
            value = cot[f * nz + z]
            g0[f, z + 1] = value
            edges_x(COT, f * nz + z, value)
            carry = edges_y(carry, f * nz + z, value)
        return carry

    carry = lax.fori_loop(0, nz, cot_layer, blank, unroll=4)
    for k in range(4):
        carry = edges_y(carry, 2 * nz + k, coef[0, k])
    ys[0, 0], ys[0, 1] = carry

    def x_copy(e, side):
        there = gx - 1 if side == 0 else gx + 1
        return pltpu.make_async_remote_copy(
            src_ref=xs.at[e, side], dst_ref=xr.at[e, 1 - side],
            send_sem=xsend.at[e, side], recv_sem=xrecv.at[e, 1 - side],
            device_id=(there, gy), device_id_type=MESH,
        )

    def y_copy(e, side):
        there = gy - 1 if side == 0 else gy + 1
        return pltpu.make_async_remote_copy(
            src_ref=ys.at[e, side], dst_ref=yr.at[e, 1 - side],
            send_sem=ysend.at[e, side], recv_sem=yrecv.at[e, 1 - side],
            device_id=(gx, there), device_id_type=MESH,
        )

    def for_sides(make, has, e, act):
        for side in range(2):
            @pl.when(has[side])
            def _():
                act(make(e, side))

    def start(c):
        c.start()

    def arrived(make, has, e):
        for side in range(2):
            @pl.when(has[side])
            def _():
                make(e, 1 - side).wait_recv()

    def block_copies(index, slot, there, mine):
        src, ssrc = (slab, scale) if mine else (slots.at[slot], sslots.at[slot])
        return [
            pltpu.make_async_remote_copy(
                src_ref=a, dst_ref=b.at[slot], send_sem=gsend.at[i, index],
                recv_sem=grecv.at[i, index], device_id=(gx, there), device_id_type=MESH,
            )
            for i, (a, b) in enumerate(((src, slots), (ssrc, sslots)))
        ]

    greeted = n_gy - 1 + jnp.where(gx > 0, 1, 0) + jnp.where(gx < n_gx - 1, 1, 0)
    pl.semaphore_wait(barrier, greeted)

    sent = []
    for k in range(1, half):
        sent += block_copies(k, gy, lax.rem(gy + 2 * k, n_gy), True)
    sent += block_copies(0, gy, partner, True)
    for c in sent:
        c.start()
    for_sides(y_copy, y_has, 0, start)
    for_sides(x_copy, x_has, COT, start)
    for k in range(1, half):
        for c in sent[2 * k - 2 : 2 * k]:
            c.wait_recv()
        onward = block_copies(half - 1 + k, lax.rem(gy - 2 * k + n_gy, n_gy), partner, False)
        for c in onward:
            c.start()
        sent += onward
    for c in sent[2 * half - 2 :]:
        c.wait_recv()
    for copy in own:
        copy.wait()

    def block_layers(index, factor, put):
        here = holder[index]
        factors = sslots[here] * factor

        def pair(p, _):
            both = slots[here, p].astype(jnp.float32)
            for j in range(2):
                l = 2 * p + j
                by = jnp.broadcast_to(to_lane(factors, l, 0)[:, 0:1], (cx, cy))
                put(l, both[j * cx : (j + 1) * cx] * by)
            return 0

        return pair

    def strength(u):
        return 1.5 + jnp.tanh(u)

    def put_own(l, value):
        f, z = l // nz, lax.rem(l, nz)
        m0[f, z + 1] = value
        edges_x(ST0, l, value)

    lax.fori_loop(0, nz, block_layers(gy, 1.0, put_own), 0, unroll=2)
    for_sides(x_copy, x_has, ST0, start)

    def put_near(ref):
        def put(l, value):
            ref[l // nz, lax.rem(l, nz)] = value
        return put

    before = block_layers(jnp.maximum(gy - 1, 0), jnp.where(gy > 0, 1.0, 0.0), put_near(left0))
    after = block_layers(jnp.minimum(gy + 1, n_gy - 1), jnp.where(gy < n_gy - 1, 1.0, 0.0), put_near(right0))

    def sides_of(p, _):
        before(p, 0)
        after(p, 0)
        return 0

    lax.fori_loop(0, nz, sides_of, 0, unroll=2)

    def strengths0(z, _):
        s = strength(m0[0, z + 1])
        m0[2, z + 1] = s
        m0[3, z + 1] = 0.75 + 0.5 * s
        left0[2, z] = strength(left0[0, z])
        right0[2, z] = strength(right0[0, z])
        return 0

    lax.fori_loop(0, nz, strengths0, 0, unroll=4)

    arrived(y_copy, y_has, 0)
    arrived(x_copy, x_has, COT)

    def beside_x(value, low, high):
        return (
            jnp.where(first_row, low, pltpu.roll(value, 1, 0)),
            jnp.where(last_row, high, pltpu.roll(value, cx - 1, 0)),
        )

    def beside_y(value, low, high, slot):
        return (
            jnp.where(first_lane, to_lane(low, slot, 0), pltpu.roll(value, 1, 1)),
            jnp.where(last_lane, to_lane(high, slot, cy - 1), pltpu.roll(value, cy - 1, 1)),
        )

    for k in range(4):
        value = coef[0, k]
        row = 2 * nz + k
        near = beside_x(value, xr[COT, 0, row], xr[COT, 1, row]) + beside_y(
            value, yr[0, 0], yr[0, 1], row
        )
        for d in range(4):
            coef[1 + d, k] = near[d]

    def near_strengths(e, side_count=2):
        for side in range(2):
            def layer(z, _):
                sx[side, z] = strength(xr[e, side, z])
                return 0
            lax.fori_loop(0, nz, layer, 0, unroll=8)

    def rows(e, row):
        return xr[e, 0, row], xr[e, 1, row]

    def state_near(level, z):
        m = m0 if level == 0 else m1
        e = ST0 if level == 0 else ST1
        found = []
        for q in range(3):
            value = m[q, z + 1]
            if q < 2:
                low, high = rows(e, q * nz + z)
            else:
                low, high = sx[0, z], sx[1, z]
            near = beside_x(value, low, high)
            if level == 0:
                near += (
                    pltpu.roll(jnp.where(last_lane, left0[q, z], value), 1, 1),
                    pltpu.roll(jnp.where(first_lane, right0[q, z], value), cy - 1, 1),
                )
            elif q < 2:
                near += beside_y(value, yr[1, 0], yr[1, 1], q * nz + z)
            else:
                near += beside_y(value, sy[0], sy[1], z)
            found.append((value,) + near)
        return found

    def forward(level, z):
        m = m0 if level == 0 else m1
        us, ts, ss = state_near(level, z)
        u, t, s = us[0], ts[0], ss[0]
        h = m[3, z + 1]
        c0, c1, c2, c3 = (coef[0, k] for k in range(4))
        kw, dtv, lamb, kv = c0 * s, c1 * h, c2 * h, c3 * s
        a = b = None
        for zn in (z, z + 2):
            x = (s + m[2, zn]) * (m[0, zn] - u)
            y = (h + m[3, zn]) * (m[1, zn] - t)
            a, b = (x, y) if a is None else (a + x, b + y)
        water, energy = c0 * a + c1 * b, c2 * b + c3 * a
        for d in range(1, 5):
            sn = ss[d]
            hn = 0.75 + 0.5 * sn
            du, dt = us[d] - u, ts[d] - t
            water += (kw + coef[d, 0] * sn) * du + (dtv + coef[d, 1] * hn) * dt
            energy += (lamb + coef[d, 2] * hn) * dt + (kv + coef[d, 3] * sn) * du
        return u + 0.5 * water, t + 0.5 * energy

    def backward(level, z):
        m, g, ge, gy_slot = (m0, g1, ADJ, 2) if level == 0 else (m1, g0, COT, 0)
        us, ts, ss = state_near(level, z)
        u, t, s = us[0], ts[0], ss[0]
        h = m[3, z + 1]
        c0, c1, c2, c3 = (coef[0, k] for k in range(4))
        kw, dtv, lamb, kv = c0 * s, c1 * h, c2 * h, c3 * s
        gws, ges = [], []
        for q, into in ((0, gws), (1, ges)):
            value = g[q, z + 1]
            into.append(value)
            into += beside_x(value, *rows(ge, q * nz + z))
            into += beside_y(value, yr[gy_slot, 0], yr[gy_slot, 1], q * nz + z)
        w, e = gws[0], ges[0]
        pu = pt = q1 = q2 = q3 = q4 = 0.0
        for zn in (z, z + 2):
            du, dt = m[0, zn] - u, m[1, zn] - t
            dw, de = g[0, zn] - w, g[1, zn] - e
            sp, hp = s + m[2, zn], h + m[3, zn]
            pu += sp * (c0 * dw + c3 * de)
            pt += hp * (c1 * dw + c2 * de)
            q1, q2, q3, q4 = q1 + du * dw, q2 + du * de, q3 + dt * dw, q4 + dt * de
        for d in range(1, 5):
            sn = ss[d]
            hn = 0.75 + 0.5 * sn
            du, dt = us[d] - u, ts[d] - t
            dw, de = gws[d] - w, ges[d] - e
            pu += (kw + coef[d, 0] * sn) * dw + (kv + coef[d, 3] * sn) * de
            pt += (dtv + coef[d, 1] * hn) * dw + (lamb + coef[d, 2] * hn) * de
            q1, q2, q3, q4 = q1 + du * dw, q2 + du * de, q3 + dt * dw, q4 + dt * de
        bend = s - 1.5
        slope = 1.0 - bend * bend
        pu -= slope * (c0 * q1 + c3 * q2 + 0.5 * (c1 * q3 + c2 * q4))
        return w + 0.5 * pu, e + 0.5 * pt

    arrived(x_copy, x_has, ST0)
    near_strengths(ST0)

    def step1(z, carry):
        pair = forward(0, z)
        for f in range(2):
            m1[f, z + 1] = pair[f]
            edges_x(ST1, f * nz + z, pair[f])
            carry = edges_y(carry, f * nz + z, pair[f])
        s = strength(pair[0])
        m1[2, z + 1] = s
        m1[3, z + 1] = 0.75 + 0.5 * s
        return carry

    ys[1, 0], ys[1, 1] = lax.fori_loop(0, nz, step1, blank, unroll=2)
    for_sides(x_copy, x_has, ST1, start)
    for_sides(y_copy, y_has, 1, start)
    arrived(x_copy, x_has, ST1)
    arrived(y_copy, y_has, 1)
    near_strengths(ST1)
    for side in range(2):
        sy[side] = strength(yr[1, side])

    def step2(z, carry):
        pair = backward(1, z)
        for f in range(2):
            g1[f, z + 1] = pair[f]
            edges_x(ADJ, f * nz + z, pair[f])
            carry = edges_y(carry, f * nz + z, pair[f])
        return carry

    ys[2, 0], ys[2, 1] = lax.fori_loop(0, nz, step2, blank, unroll=2)
    for_sides(x_copy, x_has, ADJ, start)
    for_sides(y_copy, y_has, 2, start)

    def step3(z, _):
        pair = forward(1, z)
        for f in range(2):
            out2[f * nz + z] = pair[f]
        return 0

    lax.fori_loop(0, nz, step3, 0, unroll=2)
    arrived(x_copy, x_has, ADJ)
    arrived(y_copy, y_has, 2)
    near_strengths(ST0)

    def step4(z, _):
        pair = backward(0, z)
        for f in range(2):
            outs[f * nz + z] = pair[f]
        return 0

    lax.fori_loop(0, nz, step4, 0, unroll=2)

    for c in sent:
        c.wait_send()
    for e in range(4):
        for_sides(x_copy, x_has, e, lambda c: c.wait_send())
    for e in range(3):
        for_sides(y_copy, y_has, e, lambda c: c.wait_send())


def on_device(n_gx, n_gy, stored_slab, block_scales, holder, soil_class, soil_table, cotangent):
    _, nz, cx, cy = stored_slab.shape
    layers = 2 * nz
    assert n_gy % 2 == 0 and layers + 4 <= cy
    f32 = jnp.float32
    slab = stored_slab.reshape(nz, 2 * cx, cy)
    factors = jnp.zeros((cy,), f32).at[:layers].set(block_scales.reshape(layers).astype(f32))
    factors = jnp.broadcast_to(factors[None], (cx, cy))
    cot = cotangent.reshape(layers, cx, cy)
    vmem = pl.BlockSpec(memory_space=pltpu.VMEM)
    smem = pl.BlockSpec(memory_space=pltpu.SMEM)
    out = jax.ShapeDtypeStruct((layers, cx, cy), f32)
    dma = pltpu.SemaphoreType.DMA
    state2, adjoint0 = pl.pallas_call(
        functools.partial(window, n_gx, n_gy, nz),
        out_shape=(out, out),
        in_specs=[smem, smem, vmem, vmem, vmem, vmem],
        out_specs=(vmem, vmem),
        scratch_shapes=[
            pltpu.VMEM((n_gy, nz, 2 * cx, cy), jnp.bfloat16),
            pltpu.VMEM((n_gy, cx, cy), f32),
            pltpu.VMEM((4, nz + 2, cx, cy), f32),
            pltpu.VMEM((4, nz + 2, cx, cy), f32),
            pltpu.VMEM((2, nz + 2, cx, cy), f32),
            pltpu.VMEM((2, nz + 2, cx, cy), f32),
            pltpu.VMEM((3, nz, cx, cy), f32),
            pltpu.VMEM((3, nz, cx, cy), f32),
            pltpu.VMEM((4, 2, layers + 4, 1, cy), f32),
            pltpu.VMEM((4, 2, layers + 4, 1, cy), f32),
            pltpu.VMEM((2, nz, 1, cy), f32),
            pltpu.VMEM((3, 2, cx, cy), f32),
            pltpu.VMEM((3, 2, cx, cy), f32),
            pltpu.VMEM((2, cx, cy), f32),
            pltpu.VMEM((5, 4, cx, cy), f32),
            dma((2, n_gy - 1)),
            dma((2, n_gy - 1)),
            dma((2,)),
            dma((4, 2)),
            dma((4, 2)),
            dma((3, 2)),
            dma((3, 2)),
        ],
        compiler_params=pltpu.CompilerParams(
            collective_id=0, has_side_effects=True, vmem_limit_bytes=32 * 1024 * 1024
        ),
        name="window",
    )(holder, soil_table, slab, factors, soil_class, cot)
    shape = cotangent.shape
    return state2.reshape(shape), adjoint0.reshape(shape)


def solution(mesh):
    placed = (
        P(None, None, "gx", "gy"),
        P(None, None, "gx", "gy"),
        P(),
        P("gx", "gy"),
        P(),
        P(None, None, "gx", "gy"),
    )
    return jax.shard_map(
        functools.partial(on_device, mesh.shape["gx"], mesh.shape["gy"]),
        mesh=mesh,
        in_specs=placed,
        out_specs=(P(None, None, "gx", "gy"), P(None, None, "gx", "gy")),
        check_vma=False,
    )
```

```python
import functools

import jax
import jax.numpy as jnp
from jax import lax
from jax.experimental import pallas as pl
from jax.experimental.pallas import tpu as pltpu
from jax.sharding import PartitionSpec as P

MESH = pl.DeviceIdType.MESH
COT, ST0, ST1, ADJ = range(4)


def window(
    n_gx, n_gy, nz, holder_in, table_in, slab_in, scale, classes_in, cot, out2, outs,
    holder, table, classes, slots, sslots, m0, m1, g0, g1, left0, right0, near0, near1,
    xs, xr, ys, yr, coef, gsend, grecv, lsem, xsend, xrecv, ysend, yrecv,
):
    gx, gy = lax.axis_index("gx"), lax.axis_index("gy")
    cx, cy = classes.shape
    half = n_gy // 2
    partner = gy + 1 - 2 * lax.rem(gy, 2)
    lane = lax.broadcasted_iota(jnp.int32, (cx, cy), 1)
    sub = lax.broadcasted_iota(jnp.int32, (cx, cy), 0)
    first_row, last_row = sub == 0, sub == cx - 1
    first_lane, last_lane = lane == 0, lane == cy - 1
    x_has = (gx > 0, gx < n_gx - 1)
    y_has = (gy > 0, gy < n_gy - 1)

    barrier = pltpu.get_barrier_semaphore()
    for k in range(1, n_gy):
        pl.semaphore_signal(barrier, inc=1, device_id=(gx, lax.rem(gy + k, n_gy)), device_id_type=MESH)
    for side, there in ((0, gx - 1), (1, gx + 1)):
        @pl.when(x_has[side])
        def _():
            pl.semaphore_signal(barrier, inc=1, device_id=(there, gy), device_id_type=MESH)

    small = [
        pltpu.make_async_copy(table_in, table, lsem.at[0]),
        pltpu.make_async_copy(classes_in, classes, lsem.at[1]),
        pltpu.make_async_copy(holder_in, holder, lsem.at[2]),
    ]
    own = [
        pltpu.make_async_copy(slab_in, slots.at[gy], lsem.at[3]),
        pltpu.make_async_copy(scale, sslots.at[gy], lsem.at[4]),
    ]
    cots = [
        pltpu.make_async_copy(
            cot.at[pl.ds(f * nz, nz)], g0.at[f, pl.ds(1, nz)], lsem.at[5 + f]
        )
        for f in range(2)
    ]
    for copy in small + own + cots:
        copy.start()

    for side in range(2):
        @pl.when(jnp.logical_not(x_has[side]))
        def _():
            for e in range(4):
                xr[e, side] = jnp.zeros(xr.shape[2:], jnp.float32)

        @pl.when(jnp.logical_not(y_has[side]))
        def _():
            for e in range(3):
                yr[e, side] = jnp.zeros((cx, cy), jnp.float32)

    for ref in (m0, m1, g0, g1):
        for q in range(ref.shape[0]):
            ref[q, 0] = jnp.zeros((cx, cy), jnp.float32)
            ref[q, nz + 1] = jnp.zeros((cx, cy), jnp.float32)

    def to_lane(value, lane_from, lane_to):
        return pltpu.roll(value, lax.rem(lane_to - lane_from + cy, cy), 1)

    def edges_x(e, row, value):
        xs[e, 0, row] = value[0:1]
        xs[e, 1, row] = value[cx - 1 : cx]

    def edges_y(carry, slot, value):
        low, high = carry
        here = lane == slot
        return (
            jnp.where(here, to_lane(value, 0, slot), low),
            jnp.where(here, to_lane(value, cy - 1, slot), high),
        )

    blank = (jnp.zeros((cx, cy), jnp.float32),) * 2

    def by_chunks(layers, size, work, store, carry):
        def chunk(i, carry):
            zs = [i * size + j for j in range(size)]
            found = [work(z) for z in zs]
            for z, value in zip(zs, found):
                carry = store(z, value, carry)
            return carry

        assert layers % size == 0
        return lax.fori_loop(0, layers // size, chunk, carry)

    for copy in small:
        copy.wait()
    kind = classes[...]
    for k in range(4):
        value = jnp.zeros((cx, cy), jnp.float32)
        for c in range(table.shape[1]):
            value = jnp.where(kind == c, table[k, c], value)
        coef[0, k] = value
        edges_x(COT, 2 * nz + k, value)

    def put_cot(z, values, carry):
        for f in range(2):
            edges_x(COT, f * nz + z, values[f])
            carry = edges_y(carry, f * nz + z, values[f])
        return carry

    for copy in cots:
        copy.wait()
    carry = by_chunks(nz, 8, lambda z: [g0[f, z + 1] for f in range(2)], put_cot, blank)
    for k in range(4):
        carry = edges_y(carry, 2 * nz + k, coef[0, k])
    ys[0, 0], ys[0, 1] = carry

    def x_copy(e, side):
        there = gx - 1 if side == 0 else gx + 1
        return pltpu.make_async_remote_copy(
            src_ref=xs.at[e, side], dst_ref=xr.at[e, 1 - side],
            send_sem=xsend.at[e, side], recv_sem=xrecv.at[e, 1 - side],
            device_id=(there, gy), device_id_type=MESH,
        )

    def y_copy(e, side):
        there = gy - 1 if side == 0 else gy + 1
        return pltpu.make_async_remote_copy(
            src_ref=ys.at[e, side], dst_ref=yr.at[e, 1 - side],
            send_sem=ysend.at[e, side], recv_sem=yrecv.at[e, 1 - side],
            device_id=(gx, there), device_id_type=MESH,
        )

    def for_sides(make, has, e, act):
        for side in range(2):
            @pl.when(has[side])
            def _():
                act(make(e, side))

    def start(c):
        c.start()

    def arrived(make, has, e):
        for side in range(2):
            @pl.when(has[side])
            def _():
                make(e, 1 - side).wait_recv()

    def block_copies(index, slot, there):
        src, ssrc = slots.at[slot], sslots.at[slot]
        return [
            pltpu.make_async_remote_copy(
                src_ref=a, dst_ref=b.at[slot], send_sem=gsend.at[i, index],
                recv_sem=grecv.at[i, index], device_id=(gx, there), device_id_type=MESH,
            )
            for i, (a, b) in enumerate(((src, slots), (ssrc, sslots)))
        ]

    greeted = n_gy - 1 + jnp.where(gx > 0, 1, 0) + jnp.where(gx < n_gx - 1, 1, 0)
    for copy in own:
        copy.wait()
    pl.semaphore_wait(barrier, greeted)

    sent = []
    for k in range(1, half):
        sent += block_copies(k, gy, lax.rem(gy + 2 * k, n_gy))
    sent += block_copies(0, gy, partner)
    for c in sent:
        c.start()
    for_sides(y_copy, y_has, 0, start)
    for_sides(x_copy, x_has, COT, start)
    for k in range(1, half):
        for c in sent[2 * k - 2 : 2 * k]:
            c.wait_recv()
        onward = block_copies(half - 1 + k, lax.rem(gy - 2 * k + n_gy, n_gy), partner)
        for c in onward:
            c.start()
        sent += onward
    for c in sent[2 * half - 2 :]:
        c.wait_recv()

    def strength(u):
        return 1.5 + jnp.tanh(u)

    def pair_of(index, factor):
        here = holder[index]
        factors = sslots[here] * factor

        def pair(p):
            both = slots[here, p].astype(jnp.float32)
            found = []
            for j in range(2):
                by = jnp.broadcast_to(to_lane(factors, 2 * p + j, 0)[:, 0:1], (cx, cy))
                found.append(both[j * cx : (j + 1) * cx] * by)
            return found

        return pair

    def put_own(p, values, _):
        for j in range(2):
            l = 2 * p + j
            m0[l // nz, lax.rem(l, nz) + 1] = values[j]
            edges_x(ST0, l, values[j])
        return 0

    by_chunks(nz, 8, pair_of(gy, 1.0), put_own, 0)
    for_sides(x_copy, x_has, ST0, start)

    before = pair_of(jnp.maximum(gy - 1, 0), jnp.where(gy > 0, 1.0, 0.0))
    after = pair_of(jnp.minimum(gy + 1, n_gy - 1), jnp.where(gy < n_gy - 1, 1.0, 0.0))

    def put_sides(p, values, _):
        for ref, pair in zip((left0, right0), values):
            for j in range(2):
                l = 2 * p + j
                ref[l // nz, lax.rem(l, nz)] = pair[j]
        return 0

    by_chunks(nz, 4, lambda p: (before(p), after(p)), put_sides, 0)

    def put_strength(z, s, _):
        m0[2, z + 1] = s
        m0[3, z + 1] = 0.75 + 0.5 * s
        return 0

    by_chunks(nz, 8, lambda z: strength(m0[0, z + 1]), put_strength, 0)

    arrived(y_copy, y_has, 0)
    arrived(x_copy, x_has, COT)

    def beside_x(value, low, high):
        return (
            jnp.where(first_row, low, pltpu.roll(value, 1, 0)),
            jnp.where(last_row, high, pltpu.roll(value, cx - 1, 0)),
        )

    def beside_y(value, low, high, slot):
        return (
            jnp.where(first_lane, to_lane(low, slot, 0), pltpu.roll(value, 1, 1)),
            jnp.where(last_lane, to_lane(high, slot, cy - 1), pltpu.roll(value, cy - 1, 1)),
        )

    for k in range(4):
        value = coef[0, k]
        row = 2 * nz + k
        near = beside_x(value, xr[COT, 0, row], xr[COT, 1, row]) + beside_y(
            value, yr[0, 0], yr[0, 1], row
        )
        for d in range(4):
            coef[1 + d, k] = near[d]

    def rows(e, row):
        return xr[e, 0, row], xr[e, 1, row]

    def state_near(level, z):
        m, e = (m0, ST0) if level == 0 else (m1, ST1)
        found = []
        for q in range(2):
            value = m[q, z + 1]
            near = beside_x(value, *rows(e, q * nz + z))
            if level == 0:
                near += (
                    pltpu.roll(jnp.where(last_lane, left0[q, z], value), 1, 1),
                    pltpu.roll(jnp.where(first_lane, right0[q, z], value), cy - 1, 1),
                )
            else:
                near += beside_y(value, yr[1, 0], yr[1, 1], q * nz + z)
            found.append(near)
        found.append([strength(u) for u in found[0]])
        return found

    def keep_near(ref, z, found):
        for q in range(3):
            for d in range(4):
                ref[4 * q + d, z] = found[q][d]

    def kept_near(ref, z):
        return [[ref[4 * q + d, z] for d in range(4)] for q in range(3)]

    def forward(level, z, near):
        m = m0 if level == 0 else m1
        us, ts, ss = near
        u, t, s, h = (m[q, z + 1] for q in range(4))
        c0, c1, c2, c3 = (coef[0, k] for k in range(4))
        kw, dtv, lamb, kv = c0 * s, c1 * h, c2 * h, c3 * s
        a = b = None
        for zn in (z, z + 2):
            x = (s + m[2, zn]) * (m[0, zn] - u)
            y = (h + m[3, zn]) * (m[1, zn] - t)
            a, b = (x, y) if a is None else (a + x, b + y)
        water, energy = c0 * a + c1 * b, c2 * b + c3 * a
        for d in range(4):
            sn = ss[d]
            hn = 0.75 + 0.5 * sn
            du, dt = us[d] - u, ts[d] - t
            water += (kw + coef[1 + d, 0] * sn) * du + (dtv + coef[1 + d, 1] * hn) * dt
            energy += (lamb + coef[1 + d, 2] * hn) * dt + (kv + coef[1 + d, 3] * sn) * du
        return u + 0.5 * water, t + 0.5 * energy

    def backward(level, z, near):
        m, g, ge, gy_slot = (m0, g1, ADJ, 2) if level == 0 else (m1, g0, COT, 0)
        us, ts, ss = near
        u, t, s, h = (m[q, z + 1] for q in range(4))
        c0, c1, c2, c3 = (coef[0, k] for k in range(4))
        kw, dtv, lamb, kv = c0 * s, c1 * h, c2 * h, c3 * s
        gws, ges = [], []
        for q, into in ((0, gws), (1, ges)):
            value = g[q, z + 1]
            into.append(value)
            into += beside_x(value, *rows(ge, q * nz + z))
            into += beside_y(value, yr[gy_slot, 0], yr[gy_slot, 1], q * nz + z)
        w, e = gws[0], ges[0]
        pu = pt = q1 = q2 = q3 = q4 = 0.0
        for zn in (z, z + 2):
            du, dt = m[0, zn] - u, m[1, zn] - t
            dw, de = g[0, zn] - w, g[1, zn] - e
            sp, hp = s + m[2, zn], h + m[3, zn]
            pu += sp * (c0 * dw + c3 * de)
            pt += hp * (c1 * dw + c2 * de)
            q1, q2, q3, q4 = q1 + du * dw, q2 + du * de, q3 + dt * dw, q4 + dt * de
        for d in range(4):
            sn = ss[d]
            hn = 0.75 + 0.5 * sn
            du, dt = us[d] - u, ts[d] - t
            dw, de = gws[1 + d] - w, ges[1 + d] - e
            pu += (kw + coef[1 + d, 0] * sn) * dw + (kv + coef[1 + d, 3] * sn) * de
            pt += (dtv + coef[1 + d, 1] * hn) * dw + (lamb + coef[1 + d, 2] * hn) * de
            q1, q2, q3, q4 = q1 + du * dw, q2 + du * de, q3 + dt * dw, q4 + dt * de
        bend = s - 1.5
        slope = 1.0 - bend * bend
        pu -= slope * (c0 * q1 + c3 * q2 + 0.5 * (c1 * q3 + c2 * q4))
        return w + 0.5 * pu, e + 0.5 * pt

    def put_edges(e, ref, z, pair, carry):
        for f in range(2):
            ref[f, z + 1] = pair[f]
            edges_x(e, f * nz + z, pair[f])
            carry = edges_y(carry, f * nz + z, pair[f])
        return carry

    arrived(x_copy, x_has, ST0)

    def work1(z):
        near = state_near(0, z)
        pair = forward(0, z, near)
        return near, pair, strength(pair[0])

    def put1(z, found, carry):
        near, pair, s = found
        keep_near(near0, z, near)
        m1[2, z + 1] = s
        m1[3, z + 1] = 0.75 + 0.5 * s
        return put_edges(ST1, m1, z, pair, carry)

    ys[1, 0], ys[1, 1] = by_chunks(nz, 4, work1, put1, blank)
    for_sides(x_copy, x_has, ST1, start)
    for_sides(y_copy, y_has, 1, start)
    arrived(x_copy, x_has, ST1)
    arrived(y_copy, y_has, 1)

    def work2(z):
        near = state_near(1, z)
        return near, backward(1, z, near)

    def put2(z, found, carry):
        near, pair = found
        keep_near(near1, z, near)
        return put_edges(ADJ, g1, z, pair, carry)

    ys[2, 0], ys[2, 1] = by_chunks(nz, 4, work2, put2, blank)
    for_sides(x_copy, x_has, ADJ, start)
    for_sides(y_copy, y_has, 2, start)

    def put_out(ref):
        def put(z, pair, _):
            for f in range(2):
                ref[f * nz + z] = pair[f]
            return 0
        return put

    by_chunks(nz, 4, lambda z: forward(1, z, kept_near(near1, z)), put_out(out2), 0)
    arrived(x_copy, x_has, ADJ)
    arrived(y_copy, y_has, 2)
    by_chunks(nz, 4, lambda z: backward(0, z, kept_near(near0, z)), put_out(outs), 0)

    for c in sent:
        c.wait_send()
    for e in range(4):
        for_sides(x_copy, x_has, e, lambda c: c.wait_send())
    for e in range(3):
        for_sides(y_copy, y_has, e, lambda c: c.wait_send())


def on_device(n_gx, n_gy, stored_slab, block_scales, holder, soil_class, soil_table, cotangent):
    _, nz, cx, cy = stored_slab.shape
    layers = 2 * nz
    assert n_gy % 2 == 0 and layers + 4 <= cy
    f32 = jnp.float32
    slab = stored_slab.reshape(nz, 2 * cx, cy)
    factors = jnp.zeros((cy,), f32).at[:layers].set(block_scales.reshape(layers).astype(f32))
    factors = jnp.broadcast_to(factors[None], (cx, cy))
    cot = cotangent.reshape(layers, cx, cy)
    vmem = pl.BlockSpec(memory_space=pltpu.VMEM)
    hbm = pl.BlockSpec(memory_space=pltpu.HBM)
    out = jax.ShapeDtypeStruct((layers, cx, cy), f32)
    dma = pltpu.SemaphoreType.DMA
    state2, adjoint0 = pl.pallas_call(
        functools.partial(window, n_gx, n_gy, nz),
        out_shape=(out, out),
        in_specs=[hbm, hbm, hbm, vmem, hbm, hbm],
        out_specs=(vmem, vmem),
        scratch_shapes=[
            pltpu.SMEM(holder.shape, jnp.int32),
            pltpu.SMEM(soil_table.shape[::-1], f32),
            pltpu.VMEM((cx, cy), jnp.int32),
            pltpu.VMEM((n_gy, nz, 2 * cx, cy), jnp.bfloat16),
            pltpu.VMEM((n_gy, cx, cy), f32),
            pltpu.VMEM((4, nz + 2, cx, cy), f32),
            pltpu.VMEM((4, nz + 2, cx, cy), f32),
            pltpu.VMEM((2, nz + 2, cx, cy), f32),
            pltpu.VMEM((2, nz + 2, cx, cy), f32),
            pltpu.VMEM((2, nz, cx, cy), f32),
            pltpu.VMEM((2, nz, cx, cy), f32),
            pltpu.VMEM((12, nz, cx, cy), f32),
            pltpu.VMEM((12, nz, cx, cy), f32),
            pltpu.VMEM((4, 2, layers + 4, 1, cy), f32),
            pltpu.VMEM((4, 2, layers + 4, 1, cy), f32),
            pltpu.VMEM((3, 2, cx, cy), f32),
            pltpu.VMEM((3, 2, cx, cy), f32),
            pltpu.VMEM((5, 4, cx, cy), f32),
            dma((2, n_gy - 1)),
            dma((2, n_gy - 1)),
            dma((7,)),
            dma((4, 2)),
            dma((4, 2)),
            dma((3, 2)),
            dma((3, 2)),
        ],
        compiler_params=pltpu.CompilerParams(
            collective_id=0, has_side_effects=True, vmem_limit_bytes=60 * 1024 * 1024
        ),
        name="window",
    )(holder, soil_table.T, slab, factors, soil_class, cot)
    shape = cotangent.shape
    return state2.reshape(shape), adjoint0.reshape(shape)


def solution(mesh):
    placed = (
        P(None, None, "gx", "gy"),
        P(None, None, "gx", "gy"),
        P(),
        P("gx", "gy"),
        P(),
        P(None, None, "gx", "gy"),
    )
    return jax.shard_map(
        functools.partial(on_device, mesh.shape["gx"], mesh.shape["gy"]),
        mesh=mesh,
        in_specs=placed,
        out_specs=(P(None, None, "gx", "gy"), P(None, None, "gx", "gy")),
        check_vma=False,
    )
```

```python
import functools

import jax
import jax.numpy as jnp
from jax import lax
from jax.experimental import pallas as pl
from jax.experimental.pallas import tpu as pltpu
from jax.sharding import PartitionSpec as P

MESH = pl.DeviceIdType.MESH
COT, ST0, ST1, ADJ = range(4)


def window(
    n_gx, n_gy, nz, holder_in, table_in, slab_in, scale, classes_in, cot, out2, outs,
    holder, table, classes, slots, sslots, m0, m1, g0, g1, left0, right0, near0, near1,
    gnear, held2, helds, xs, xr, ys, yr, coef,
    gsend, grecv, lsem, osem, xsend, xrecv, ysend, yrecv,
):
    gx, gy = lax.axis_index("gx"), lax.axis_index("gy")
    cx, cy = classes.shape
    chips, hz = n_gy // 2, nz // 2
    partner = gy + 1 - 2 * lax.rem(gy, 2)
    lane = lax.broadcasted_iota(jnp.int32, (cx, cy), 1)
    sub = lax.broadcasted_iota(jnp.int32, (cx, cy), 0)
    first_row, last_row = sub == 0, sub == cx - 1
    first_lane, last_lane = lane == 0, lane == cy - 1
    x_has = (gx > 0, gx < n_gx - 1)
    y_has = (gy > 0, gy < n_gy - 1)

    barrier = pltpu.get_barrier_semaphore()
    for k in range(1, n_gy):
        pl.semaphore_signal(barrier, inc=1, device_id=(gx, lax.rem(gy + k, n_gy)), device_id_type=MESH)
    for side, there in ((0, gx - 1), (1, gx + 1)):
        @pl.when(x_has[side])
        def _():
            pl.semaphore_signal(barrier, inc=1, device_id=(there, gy), device_id_type=MESH)

    small = [
        pltpu.make_async_copy(table_in, table, lsem.at[0]),
        pltpu.make_async_copy(classes_in, classes, lsem.at[1]),
        pltpu.make_async_copy(holder_in, holder, lsem.at[2]),
    ]
    own = [
        pltpu.make_async_copy(slab_in, slots.at[gy], lsem.at[3]),
        pltpu.make_async_copy(scale, sslots.at[gy], lsem.at[4]),
    ]
    cots = [
        pltpu.make_async_copy(
            cot.at[pl.ds(f * nz, nz)], g0.at[f, pl.ds(1, nz)], lsem.at[5 + f]
        )
        for f in range(2)
    ]
    for copy in small + own + cots:
        copy.start()

    for side in range(2):
        @pl.when(jnp.logical_not(x_has[side]))
        def _():
            for e in range(4):
                xr[e, side] = jnp.zeros(xr.shape[2:], jnp.float32)

        @pl.when(jnp.logical_not(y_has[side]))
        def _():
            for e in range(3):
                for half in range(2):
                    yr[e, half, side] = jnp.zeros((cx, cy), jnp.float32)

    def row_of(f, z):
        return z + f * hz + lax.div(z, hz) * hz

    for ref in (m0, m1, g0, g1):
        for q in range(ref.shape[0]):
            ref[q, 0] = jnp.zeros((cx, cy), jnp.float32)
            ref[q, nz + 1] = jnp.zeros((cx, cy), jnp.float32)

    def to_lane(value, lane_from, lane_to):
        return pltpu.roll(value, lax.rem(lane_to - lane_from + cy, cy), 1)

    def edges_x(e, row, value):
        xs[e, 0, row] = value[0:1]
        xs[e, 1, row] = value[cx - 1 : cx]

    def edges_y(carry, slot, value):
        low, high = carry
        here = lane == slot
        return (
            jnp.where(here, to_lane(value, 0, slot), low),
            jnp.where(here, to_lane(value, cy - 1, slot), high),
        )

    blank = (jnp.zeros((cx, cy), jnp.float32),) * 2

    def by_chunks(first, layers, size, work, store, carry):
        def chunk(i, carry):
            zs = [first + i * size + j for j in range(size)]
            found = [work(z) for z in zs]
            for z, value in zip(zs, found):
                carry = store(z, value, carry)
            return carry

        assert layers % size == 0
        return lax.fori_loop(0, layers // size, chunk, carry)

    for copy in small:
        copy.wait()
    kind = classes[...]
    for k in range(4):
        value = jnp.zeros((cx, cy), jnp.float32)
        for c in range(table.shape[1]):
            value = jnp.where(kind == c, table[k, c], value)
        coef[0, k] = value
        edges_x(COT, 2 * nz + k, value)

    def put_cot(z, values, carry):
        for f in range(2):
            edges_x(COT, row_of(f, z), values[f])
            carry = edges_y(carry, row_of(f, z), values[f])
        return carry

    for copy in cots:
        copy.wait()
    carry = by_chunks(0, nz, 8, lambda z: [g0[f, z + 1] for f in range(2)], put_cot, blank)
    for k in range(4):
        carry = edges_y(carry, 2 * nz + k, coef[0, k])
    ys[0, 0, 0], ys[0, 0, 1] = carry

    def x_copy(e, half, side):
        there = gx - 1 if side == 0 else gx + 1
        part = pl.ds(0, 2 * nz + 4) if e == COT else pl.ds(half * nz, nz)
        return pltpu.make_async_remote_copy(
            src_ref=xs.at[e, side, part], dst_ref=xr.at[e, 1 - side, part],
            send_sem=xsend.at[e, half, side], recv_sem=xrecv.at[e, half, 1 - side],
            device_id=(there, gy), device_id_type=MESH,
        )

    y_of = {COT: 0, ST1: 1, ADJ: 2}

    def y_copy(e, half, side):
        there = gy - 1 if side == 0 else gy + 1
        i = y_of[e]
        return pltpu.make_async_remote_copy(
            src_ref=ys.at[i, half, side], dst_ref=yr.at[i, half, 1 - side],
            send_sem=ysend.at[i, half, side], recv_sem=yrecv.at[i, half, 1 - side],
            device_id=(gx, there), device_id_type=MESH,
        )

    def each(e, half, act, mirrored=False):
        for make, has in ((x_copy, x_has), (y_copy, y_has)):
            if make is y_copy and e not in y_of:
                continue
            for side in range(2):
                @pl.when(has[side])
                def _():
                    act(make(e, half, 1 - side if mirrored else side))

    def start(e, half):
        each(e, half, lambda c: c.start())

    def arrived(e, half):
        each(e, half, lambda c: c.wait_recv(), mirrored=True)

    def block_copies(index, slot, there, field):
        part = pl.ds(field * hz, hz)
        pieces = [(slots.at[slot, part], field)]
        if field == 0:
            pieces.append((sslots.at[slot], 2))
        return [
            pltpu.make_async_remote_copy(
                src_ref=ref, dst_ref=ref, send_sem=gsend.at[i, index],
                recv_sem=grecv.at[i, index], device_id=(gx, there), device_id_type=MESH,
            )
            for ref, i in pieces
        ]

    greeted = n_gy - 1 + jnp.where(gx > 0, 1, 0) + jnp.where(gx < n_gx - 1, 1, 0)
    for copy in own:
        copy.wait()
    pl.semaphore_wait(barrier, greeted)

    start(COT, 0)
    direct = [
        [block_copies(k, gy, lax.rem(gy + 2 * k, n_gy), field) for k in range(1, chips)]
        for field in range(2)
    ]
    beside = [block_copies(0, gy, partner, field) for field in range(2)]
    for field in range(2):
        for copies in direct[field] + [beside[field]]:
            for c in copies:
                c.start()
    sent = direct[0] + direct[1] + beside
    onward = [[], []]

    def pass_on(field):
        for k in range(1, chips):
            for c in direct[field][k - 1]:
                c.wait_recv()
            copies = block_copies(chips - 1 + k, lax.rem(gy - 2 * k + n_gy, n_gy), partner, field)
            for c in copies:
                c.start()
            onward[field].append(copies)

    arrived(COT, 0)

    def beside_x(value, low, high):
        return (
            jnp.where(first_row, low, pltpu.roll(value, 1, 0)),
            jnp.where(last_row, high, pltpu.roll(value, cx - 1, 0)),
        )

    def beside_y(value, low, high, slot):
        return (
            jnp.where(first_lane, to_lane(low, slot, 0), pltpu.roll(value, 1, 1)),
            jnp.where(last_lane, to_lane(high, slot, cy - 1), pltpu.roll(value, cy - 1, 1)),
        )

    for k in range(4):
        value = coef[0, k]
        row = 2 * nz + k
        near = beside_x(value, xr[COT, 0, row], xr[COT, 1, row]) + beside_y(
            value, yr[0, 0, 0], yr[0, 0, 1], row
        )
        for d in range(4):
            coef[1 + d, k] = near[d]

    def rows(e, row):
        return xr[e, 0, row], xr[e, 1, row]

    def field_near(e, f, z, value):
        row, i, half = row_of(f, z), y_of[e], 0 if e == COT else lax.div(z, hz)
        return beside_x(value, *rows(e, row)) + beside_y(value, yr[i, half, 0], yr[i, half, 1], row)

    def put_cot_near(z, found, _):
        for f in range(2):
            for d in range(4):
                gnear[4 * f + d, z] = found[f][d]
        return 0

    by_chunks(0, nz, 4, lambda z: [field_near(COT, f, z, g0[f, z + 1]) for f in range(2)], put_cot_near, 0)

    for field in range(2):
        pass_on(field)
    sent += onward[0] + onward[1]
    for copies in beside + onward[0] + onward[1]:
        for c in copies:
            c.wait_recv()

    def strength(u):
        return 1.5 + jnp.tanh(u)

    def pair_of(index, factor):
        here = holder[index]
        factors = sslots[here] * factor

        def pair(p):
            both = slots[here, p].astype(jnp.float32)
            found = []
            for j in range(2):
                by = jnp.broadcast_to(to_lane(factors, 2 * p + j, 0)[:, 0:1], (cx, cy))
                found.append(both[j * cx : (j + 1) * cx] * by)
            return found

        return pair

    def put_own(p, found, _):
        values, strengths = found
        for j in range(2):
            l = 2 * p + j
            f, z = lax.div(l, nz), lax.rem(l, nz)
            m0[f, z + 1] = values[j]
            edges_x(ST0, row_of(f, z), values[j])
            if strengths:
                m0[2, z + 1] = strengths[j]
                m0[3, z + 1] = 0.75 + 0.5 * strengths[j]
        return 0

    def own_of(f):
        pair = pair_of(gy, 1.0)

        def work(p):
            values = pair(p)
            return values, [strength(v) for v in values] if f == 0 else None

        return work

    quarter = hz // 2
    for half in range(2):
        for f in range(2):
            by_chunks(f * hz + half * quarter, quarter, 8, own_of(f), put_own, 0)
        start(ST0, half)

    before = pair_of(jnp.maximum(gy - 1, 0), jnp.where(gy > 0, 1.0, 0.0))
    after = pair_of(jnp.minimum(gy + 1, n_gy - 1), jnp.where(gy < n_gy - 1, 1.0, 0.0))

    def put_sides(p, values, _):
        for ref, pair in zip((left0, right0), values):
            for j in range(2):
                l = 2 * p + j
                ref[l // nz, lax.rem(l, nz)] = pair[j]
        return 0

    by_chunks(0, nz, 4, lambda p: (before(p), after(p)), put_sides, 0)

    def state_near(level, z):
        m, e = (m0, ST0) if level == 0 else (m1, ST1)
        found = []
        for q in range(2):
            value = m[q, z + 1]
            if level == 0:
                near = beside_x(value, *rows(e, row_of(q, z))) + (
                    pltpu.roll(jnp.where(last_lane, left0[q, z], value), 1, 1),
                    pltpu.roll(jnp.where(first_lane, right0[q, z], value), cy - 1, 1),
                )
            else:
                near = field_near(ST1, q, z, value)
            found.append(near)
        found.append([strength(u) for u in found[0]])
        return found

    def keep_near(ref, z, found):
        for q in range(3):
            for d in range(4):
                ref[4 * q + d, z] = found[q][d]

    def kept_near(ref, z):
        return [[ref[4 * q + d, z] for d in range(4)] for q in range(3)]

    def forward(level, z, near):
        m = m0 if level == 0 else m1
        us, ts, ss = near
        u, t, s, h = (m[q, z + 1] for q in range(4))
        c0, c1, c2, c3 = (coef[0, k] for k in range(4))
        kw, dtv, lamb, kv = c0 * s, c1 * h, c2 * h, c3 * s
        a = b = None
        for zn in (z, z + 2):
            x = (s + m[2, zn]) * (m[0, zn] - u)
            y = (h + m[3, zn]) * (m[1, zn] - t)
            a, b = (x, y) if a is None else (a + x, b + y)
        water, energy = c0 * a + c1 * b, c2 * b + c3 * a
        for d in range(4):
            sn = ss[d]
            hn = 0.75 + 0.5 * sn
            du, dt = us[d] - u, ts[d] - t
            water += (kw + coef[1 + d, 0] * sn) * du + (dtv + coef[1 + d, 1] * hn) * dt
            energy += (lamb + coef[1 + d, 2] * hn) * dt + (kv + coef[1 + d, 3] * sn) * du
        return u + 0.5 * water, t + 0.5 * energy

    def backward(level, z, near):
        m, g = (m0, g1) if level == 0 else (m1, g0)
        us, ts, ss = near
        u, t, s, h = (m[q, z + 1] for q in range(4))
        c0, c1, c2, c3 = (coef[0, k] for k in range(4))
        kw, dtv, lamb, kv = c0 * s, c1 * h, c2 * h, c3 * s
        w, e = g[0, z + 1], g[1, z + 1]
        if level == 0:
            gws, ges = field_near(ADJ, 0, z, w), field_near(ADJ, 1, z, e)
        else:
            gws, ges = ([gnear[4 * f + d, z] for d in range(4)] for f in range(2))
        pu = pt = q1 = q2 = q3 = q4 = 0.0
        for zn in (z, z + 2):
            du, dt = m[0, zn] - u, m[1, zn] - t
            dw, de = g[0, zn] - w, g[1, zn] - e
            sp, hp = s + m[2, zn], h + m[3, zn]
            pu += sp * (c0 * dw + c3 * de)
            pt += hp * (c1 * dw + c2 * de)
            q1, q2, q3, q4 = q1 + du * dw, q2 + du * de, q3 + dt * dw, q4 + dt * de
        for d in range(4):
            sn = ss[d]
            hn = 0.75 + 0.5 * sn
            du, dt = us[d] - u, ts[d] - t
            dw, de = gws[d] - w, ges[d] - e
            pu += (kw + coef[1 + d, 0] * sn) * dw + (kv + coef[1 + d, 3] * sn) * de
            pt += (dtv + coef[1 + d, 1] * hn) * dw + (lamb + coef[1 + d, 2] * hn) * de
            q1, q2, q3, q4 = q1 + du * dw, q2 + du * de, q3 + dt * dw, q4 + dt * de
        bend = s - 1.5
        slope = 1.0 - bend * bend
        pu -= slope * (c0 * q1 + c3 * q2 + 0.5 * (c1 * q3 + c2 * q4))
        return w + 0.5 * pu, e + 0.5 * pt

    def put_edges(e, ref, z, pair, carry):
        for f in range(2):
            ref[f, z + 1] = pair[f]
            edges_x(e, row_of(f, z), pair[f])
            carry = edges_y(carry, row_of(f, z), pair[f])
        return carry

    def work1(z):
        near = state_near(0, z)
        pair = forward(0, z, near)
        return near, pair, strength(pair[0])

    def put1(z, found, carry):
        near, pair, s = found
        keep_near(near0, z, near)
        m1[2, z + 1] = s
        m1[3, z + 1] = 0.75 + 0.5 * s
        return put_edges(ST1, m1, z, pair, carry)

    for half in range(2):
        arrived(ST0, half)
        ys[1, half, 0], ys[1, half, 1] = by_chunks(half * hz, hz, 4, work1, put1, blank)
        start(ST1, half)

    def work2(z):
        near = state_near(1, z)
        return near, backward(1, z, near)

    def put2(z, found, carry):
        near, pair = found
        keep_near(near1, z, near)
        return put_edges(ADJ, g1, z, pair, carry)

    for half in range(2):
        arrived(ST1, half)
        ys[2, half, 0], ys[2, half, 1] = by_chunks(half * hz, hz, 4, work2, put2, blank)
        start(ADJ, half)

    def put_out(ref):
        def put(z, pair, _):
            for f in range(2):
                ref[f * nz + z] = pair[f]
            return 0
        return put

    written = []

    def write(i, held, out, half):
        for f in range(2):
            part = pl.ds(f * nz + half * hz, hz)
            copy = pltpu.make_async_copy(held.at[part], out.at[part], osem.at[i, half, f])
            copy.start()
            written.append(copy)

    for half in range(2):
        by_chunks(
            half * hz, hz, 4, lambda z: forward(1, z, kept_near(near1, z)), put_out(held2), 0
        )
        write(0, held2, out2, half)
    for half in range(2):
        arrived(ADJ, half)
        by_chunks(
            half * hz, hz, 4, lambda z: backward(0, z, kept_near(near0, z)), put_out(helds), 0
        )
        write(1, helds, outs, half)

    for copies in sent:
        for c in copies:
            c.wait_send()
    each(COT, 0, lambda c: c.wait_send())
    for e in (ST0, ST1, ADJ):
        for half in range(2):
            each(e, half, lambda c: c.wait_send())
    for copy in written:
        copy.wait()


def hand_over(a, b, a_out, b_out, sems):
    layers, parts = a.shape[0], sems.shape[1]
    copies = [
        pltpu.make_async_copy(
            src.at[pl.ds(j * layers // parts, layers // parts)],
            dst.at[pl.ds(j * layers // parts, layers // parts)],
            sems.at[i, j],
        )
        for i, (src, dst) in enumerate(((a, a_out), (b, b_out)))
        for j in range(parts)
    ]
    for c in copies:
        c.start()
    for c in copies:
        c.wait()


def on_device(n_gx, n_gy, stored_slab, block_scales, holder, soil_class, soil_table, cotangent):
    _, nz, cx, cy = stored_slab.shape
    layers = 2 * nz
    assert n_gy % 2 == 0 and layers + 4 <= cy
    f32 = jnp.float32
    slab = stored_slab.reshape(nz, 2 * cx, cy)
    factors = jnp.zeros((cy,), f32).at[:layers].set(block_scales.reshape(layers).astype(f32))
    factors = jnp.broadcast_to(factors[None], (cx, cy))
    cot = cotangent.reshape(layers, cx, cy)
    vmem = pl.BlockSpec(memory_space=pltpu.VMEM)
    hbm = pl.BlockSpec(memory_space=pltpu.HBM)
    out = jax.ShapeDtypeStruct((layers, cx, cy), f32)
    dma = pltpu.SemaphoreType.DMA
    state2, adjoint0 = pl.pallas_call(
        functools.partial(window, n_gx, n_gy, nz),
        out_shape=(out, out),
        in_specs=[hbm, hbm, hbm, vmem, hbm, hbm],
        out_specs=(hbm, hbm),
        scratch_shapes=[
            pltpu.SMEM(holder.shape, jnp.int32),
            pltpu.SMEM(soil_table.shape[::-1], f32),
            pltpu.VMEM((cx, cy), jnp.int32),
            pltpu.VMEM((n_gy, nz, 2 * cx, cy), jnp.bfloat16),
            pltpu.VMEM((n_gy, cx, cy), f32),
            pltpu.VMEM((4, nz + 2, cx, cy), f32),
            pltpu.VMEM((4, nz + 2, cx, cy), f32),
            pltpu.VMEM((2, nz + 2, cx, cy), f32),
            pltpu.VMEM((2, nz + 2, cx, cy), f32),
            pltpu.VMEM((2, nz, cx, cy), f32),
            pltpu.VMEM((2, nz, cx, cy), f32),
            pltpu.VMEM((12, nz, cx, cy), f32),
            pltpu.VMEM((12, nz, cx, cy), f32),
            pltpu.VMEM((8, nz, cx, cy), f32),
            pltpu.VMEM((layers, cx, cy), f32),
            pltpu.VMEM((layers, cx, cy), f32),
            pltpu.VMEM((4, 2, layers + 4, 1, cy), f32),
            pltpu.VMEM((4, 2, layers + 4, 1, cy), f32),
            pltpu.VMEM((3, 2, 2, cx, cy), f32),
            pltpu.VMEM((3, 2, 2, cx, cy), f32),
            pltpu.VMEM((5, 4, cx, cy), f32),
            dma((3, n_gy - 1)),
            dma((3, n_gy - 1)),
            dma((7,)),
            dma((2, 2, 2)),
            dma((4, 2, 2)),
            dma((4, 2, 2)),
            dma((3, 2, 2)),
            dma((3, 2, 2)),
        ],
        compiler_params=pltpu.CompilerParams(
            collective_id=0, has_side_effects=True, vmem_limit_bytes=60 * 1024 * 1024
        ),
        name="window",
    )(holder, soil_table.T, slab, factors, soil_class, cot)
    state2, adjoint0 = pl.pallas_call(
        hand_over,
        out_shape=(out, out),
        in_specs=[hbm, hbm],
        out_specs=(hbm, hbm),
        scratch_shapes=[dma((2, 4))],
        compiler_params=pltpu.CompilerParams(vmem_limit_bytes=60 * 1024 * 1024),
        name="hand_over",
    )(state2, adjoint0)
    shape = cotangent.shape
    return state2.reshape(shape), adjoint0.reshape(shape)


def solution(mesh):
    placed = (
        P(None, None, "gx", "gy"),
        P(None, None, "gx", "gy"),
        P(),
        P("gx", "gy"),
        P(),
        P(None, None, "gx", "gy"),
    )
    return jax.shard_map(
        functools.partial(on_device, mesh.shape["gx"], mesh.shape["gy"]),
        mesh=mesh,
        in_specs=placed,
        out_specs=(P(None, None, "gx", "gy"), P(None, None, "gx", "gy")),
        check_vma=False,
    )
```

```python
import functools

import jax
import jax.numpy as jnp
from jax import lax
from jax.experimental import pallas as pl
from jax.experimental.pallas import tpu as pltpu
from jax.sharding import PartitionSpec as P

MESH = pl.DeviceIdType.MESH
COT, ST0, ST1, ADJ = range(4)


def window(
    n_gx, n_gy, nz, holder_in, table_in, slab_in, scale, classes_in, cot, out2, outs,
    holder, table, classes, scales, spread, slots, sslots, m0, m1, g0, g1, left0, right0, near0, near1,
    gnear, held2, helds, xs, xr, ys, yr, coef,
    gsend, grecv, lsem, osem, xsend, xrecv, ysend, yrecv,
):
    gx, gy = lax.axis_index("gx"), lax.axis_index("gy")
    cx, cy = classes.shape
    chips, hz = n_gy // 2, nz // 2
    partner = gy + 1 - 2 * lax.rem(gy, 2)
    lane = lax.broadcasted_iota(jnp.int32, (cx, cy), 1)
    sub = lax.broadcasted_iota(jnp.int32, (cx, cy), 0)
    first_row, last_row = sub == 0, sub == cx - 1
    first_lane, last_lane = lane == 0, lane == cy - 1
    x_has = (gx > 0, gx < n_gx - 1)
    y_has = (gy > 0, gy < n_gy - 1)

    barrier = pltpu.get_barrier_semaphore()
    for k in range(1, n_gy):
        pl.semaphore_signal(barrier, inc=1, device_id=(gx, lax.rem(gy + k, n_gy)), device_id_type=MESH)
    for side, there in ((0, gx - 1), (1, gx + 1)):
        @pl.when(x_has[side])
        def _():
            pl.semaphore_signal(barrier, inc=1, device_id=(there, gy), device_id_type=MESH)

    small = [
        pltpu.make_async_copy(table_in, table, lsem.at[0]),
        pltpu.make_async_copy(classes_in, classes, lsem.at[1]),
        pltpu.make_async_copy(holder_in, holder, lsem.at[2]),
    ]
    own = [
        pltpu.make_async_copy(slab_in, slots.at[gy], lsem.at[3]),
    ]
    scaling = pltpu.make_async_copy(scale, scales, lsem.at[4])
    cots = [
        pltpu.make_async_copy(
            cot.at[pl.ds(f * nz, nz)], g0.at[f, pl.ds(1, nz)], lsem.at[5 + f]
        )
        for f in range(2)
    ]
    for copy in own + [scaling] + small + cots:
        copy.start()
    greeted = n_gy - 1 + jnp.where(gx > 0, 1, 0) + jnp.where(gx < n_gx - 1, 1, 0)
    pl.semaphore_wait(barrier, greeted)

    def block_copies(index, slot, there, field):
        part = pl.ds(field * hz, hz)
        src = slab_in.at[part] if slot is gy else slots.at[slot, part]
        pieces = [(src, slots.at[slot, part], field)]
        if field == 1:
            pieces.append((sslots.at[slot], sslots.at[slot], 2))
        return [
            pltpu.make_async_remote_copy(
                src_ref=src, dst_ref=dst, send_sem=gsend.at[i, index],
                recv_sem=grecv.at[i, index], device_id=(gx, there), device_id_type=MESH,
            )
            for src, dst, i in pieces
        ]

    direct = [
        [block_copies(k, gy, lax.rem(gy + 2 * k, n_gy), field) for k in range(1, chips)]
        for field in range(2)
    ]
    beside = [block_copies(0, gy, partner, field) for field in range(2)]
    for field in range(2):
        for copies in direct[field] + [beside[field]]:
            copies[0].start()
    spread[...] = jnp.zeros((cx, cy), jnp.float32)
    scaling.wait()
    spread[0:2, 0:nz] = scales[...].astype(jnp.float32)
    sslots[gy] = jnp.where(
        lane < nz,
        jnp.broadcast_to(spread[0:1], (cx, cy)),
        pltpu.roll(jnp.broadcast_to(spread[1:2], (cx, cy)), nz, 1),
    )
    for copies in direct[1] + [beside[1]]:
        copies[1].start()

    for side in range(2):
        @pl.when(jnp.logical_not(x_has[side]))
        def _():
            for e in range(4):
                xr[e, side] = jnp.zeros(xr.shape[2:], jnp.float32)

        @pl.when(jnp.logical_not(y_has[side]))
        def _():
            for e in range(3):
                for half in range(2):
                    yr[e, half, side] = jnp.zeros((cx, cy), jnp.float32)

    def row_of(f, z):
        return z + f * hz + lax.div(z, hz) * hz

    for ref in (m0, m1, g0, g1):
        for q in range(ref.shape[0]):
            ref[q, 0] = jnp.zeros((cx, cy), jnp.float32)
            ref[q, nz + 1] = jnp.zeros((cx, cy), jnp.float32)

    def to_lane(value, lane_from, lane_to):
        return pltpu.roll(value, lax.rem(lane_to - lane_from + cy, cy), 1)

    def edges_x(e, row, value):
        xs[e, 0, row] = value[0:1]
        xs[e, 1, row] = value[cx - 1 : cx]

    def edges_y(carry, slot, value):
        low, high = carry
        here = lane == slot
        return (
            jnp.where(here, to_lane(value, 0, slot), low),
            jnp.where(here, to_lane(value, cy - 1, slot), high),
        )

    blank = (jnp.zeros((cx, cy), jnp.float32),) * 2

    def by_chunks(first, layers, size, work, store, carry):
        def chunk(i, carry):
            zs = [first + i * size + j for j in range(size)]
            found = [work(z) for z in zs]
            for z, value in zip(zs, found):
                carry = store(z, value, carry)
            return carry

        assert layers % size == 0
        return lax.fori_loop(0, layers // size, chunk, carry)

    for copy in small:
        copy.wait()
    kind = classes[...]
    for k in range(4):
        value = jnp.zeros((cx, cy), jnp.float32)
        for c in range(table.shape[1]):
            value = jnp.where(kind == c, table[k, c], value)
        coef[0, k] = value
        edges_x(COT, 2 * nz + k, value)

    def put_cot(z, values, carry):
        for f in range(2):
            edges_x(COT, row_of(f, z), values[f])
            carry = edges_y(carry, row_of(f, z), values[f])
        return carry

    for copy in cots:
        copy.wait()
    carry = by_chunks(0, nz, 8, lambda z: [g0[f, z + 1] for f in range(2)], put_cot, blank)
    for k in range(4):
        carry = edges_y(carry, 2 * nz + k, coef[0, k])
    ys[0, 0, 0], ys[0, 0, 1] = carry

    def x_copy(e, half, side):
        there = gx - 1 if side == 0 else gx + 1
        part = pl.ds(0, 2 * nz + 4) if e == COT else pl.ds(half * nz, nz)
        return pltpu.make_async_remote_copy(
            src_ref=xs.at[e, side, part], dst_ref=xr.at[e, 1 - side, part],
            send_sem=xsend.at[e, half, side], recv_sem=xrecv.at[e, half, 1 - side],
            device_id=(there, gy), device_id_type=MESH,
        )

    y_of = {COT: 0, ST1: 1, ADJ: 2}

    def y_copy(e, half, side):
        there = gy - 1 if side == 0 else gy + 1
        i = y_of[e]
        return pltpu.make_async_remote_copy(
            src_ref=ys.at[i, half, side], dst_ref=yr.at[i, half, 1 - side],
            send_sem=ysend.at[i, half, side], recv_sem=yrecv.at[i, half, 1 - side],
            device_id=(gx, there), device_id_type=MESH,
        )

    def each(e, half, act, mirrored=False):
        for make, has in ((x_copy, x_has), (y_copy, y_has)):
            if make is y_copy and e not in y_of:
                continue
            for side in range(2):
                @pl.when(has[side])
                def _():
                    act(make(e, half, 1 - side if mirrored else side))

    def start(e, half):
        each(e, half, lambda c: c.start())

    def arrived(e, half):
        each(e, half, lambda c: c.wait_recv(), mirrored=True)

    start(COT, 0)
    sent = direct[0] + direct[1] + beside
    onward = [[], []]

    def pass_on(field):
        for k in range(1, chips):
            for c in direct[field][k - 1]:
                c.wait_recv()
            copies = block_copies(chips - 1 + k, lax.rem(gy - 2 * k + n_gy, n_gy), partner, field)
            for c in copies:
                c.start()
            onward[field].append(copies)

    for field in range(2):
        pass_on(field)

    arrived(COT, 0)

    def beside_x(value, low, high):
        return (
            jnp.where(first_row, low, pltpu.roll(value, 1, 0)),
            jnp.where(last_row, high, pltpu.roll(value, cx - 1, 0)),
        )

    def beside_y(value, low, high, slot):
        return (
            jnp.where(first_lane, to_lane(low, slot, 0), pltpu.roll(value, 1, 1)),
            jnp.where(last_lane, to_lane(high, slot, cy - 1), pltpu.roll(value, cy - 1, 1)),
        )

    for k in range(4):
        value = coef[0, k]
        row = 2 * nz + k
        near = beside_x(value, xr[COT, 0, row], xr[COT, 1, row]) + beside_y(
            value, yr[0, 0, 0], yr[0, 0, 1], row
        )
        for d in range(4):
            coef[1 + d, k] = near[d]

    def rows(e, row):
        return xr[e, 0, row], xr[e, 1, row]

    def field_near(e, f, z, value):
        row, i, half = row_of(f, z), y_of[e], 0 if e == COT else lax.div(z, hz)
        return beside_x(value, *rows(e, row)) + beside_y(value, yr[i, half, 0], yr[i, half, 1], row)

    def put_cot_near(z, found, _):
        for f in range(2):
            for d in range(4):
                gnear[4 * f + d, z] = found[f][d]
        return 0

    by_chunks(0, nz, 4, lambda z: [field_near(COT, f, z, g0[f, z + 1]) for f in range(2)], put_cot_near, 0)

    sent += onward[0] + onward[1]
    for copies in beside + onward[0] + onward[1]:
        for c in copies:
            c.wait_recv()
    for copy in own:
        copy.wait()

    def strength(u):
        return 1.5 + jnp.tanh(u)

    def pair_of(index, factor):
        here = holder[index]
        factors = sslots[here] * factor

        def pair(p):
            both = slots[here, p].astype(jnp.float32)
            found = []
            for j in range(2):
                by = jnp.broadcast_to(to_lane(factors, 2 * p + j, 0)[:, 0:1], (cx, cy))
                found.append(both[j * cx : (j + 1) * cx] * by)
            return found

        return pair

    def put_own(p, found, _):
        values, strengths = found
        for j in range(2):
            l = 2 * p + j
            f, z = lax.div(l, nz), lax.rem(l, nz)
            m0[f, z + 1] = values[j]
            edges_x(ST0, row_of(f, z), values[j])
            if strengths:
                m0[2, z + 1] = strengths[j]
                m0[3, z + 1] = 0.75 + 0.5 * strengths[j]
        return 0

    def own_of(f):
        pair = pair_of(gy, 1.0)

        def work(p):
            values = pair(p)
            return values, [strength(v) for v in values] if f == 0 else None

        return work

    quarter = hz // 2
    for half in range(2):
        for f in range(2):
            by_chunks(f * hz + half * quarter, quarter, 8, own_of(f), put_own, 0)
        start(ST0, half)

    before = pair_of(jnp.maximum(gy - 1, 0), jnp.where(gy > 0, 1.0, 0.0))
    after = pair_of(jnp.minimum(gy + 1, n_gy - 1), jnp.where(gy < n_gy - 1, 1.0, 0.0))

    def put_sides(p, values, _):
        for ref, pair in zip((left0, right0), values):
            for j in range(2):
                l = 2 * p + j
                ref[l // nz, lax.rem(l, nz)] = pair[j]
        return 0

    by_chunks(0, nz, 4, lambda p: (before(p), after(p)), put_sides, 0)

    def state_near(level, z):
        m, e = (m0, ST0) if level == 0 else (m1, ST1)
        found = []
        for q in range(2):
            value = m[q, z + 1]
            if level == 0:
                near = beside_x(value, *rows(e, row_of(q, z))) + (
                    pltpu.roll(jnp.where(last_lane, left0[q, z], value), 1, 1),
                    pltpu.roll(jnp.where(first_lane, right0[q, z], value), cy - 1, 1),
                )
            else:
                near = field_near(ST1, q, z, value)
            found.append(near)
        found.append([strength(u) for u in found[0]])
        return found

    def keep_near(ref, z, found):
        for q in range(3):
            for d in range(4):
                ref[4 * q + d, z] = found[q][d]

    def kept_near(ref, z):
        return [[ref[4 * q + d, z] for d in range(4)] for q in range(3)]

    def forward(level, z, near):
        m = m0 if level == 0 else m1
        us, ts, ss = near
        u, t, s, h = (m[q, z + 1] for q in range(4))
        c0, c1, c2, c3 = (coef[0, k] for k in range(4))
        kw, dtv, lamb, kv = c0 * s, c1 * h, c2 * h, c3 * s
        a = b = None
        for zn in (z, z + 2):
            x = (s + m[2, zn]) * (m[0, zn] - u)
            y = (h + m[3, zn]) * (m[1, zn] - t)
            a, b = (x, y) if a is None else (a + x, b + y)
        water, energy = c0 * a + c1 * b, c2 * b + c3 * a
        for d in range(4):
            sn = ss[d]
            hn = 0.75 + 0.5 * sn
            du, dt = us[d] - u, ts[d] - t
            water += (kw + coef[1 + d, 0] * sn) * du + (dtv + coef[1 + d, 1] * hn) * dt
            energy += (lamb + coef[1 + d, 2] * hn) * dt + (kv + coef[1 + d, 3] * sn) * du
        return u + 0.5 * water, t + 0.5 * energy

    def backward(level, z, near):
        m, g = (m0, g1) if level == 0 else (m1, g0)
        us, ts, ss = near
        u, t, s, h = (m[q, z + 1] for q in range(4))
        c0, c1, c2, c3 = (coef[0, k] for k in range(4))
        kw, dtv, lamb, kv = c0 * s, c1 * h, c2 * h, c3 * s
        w, e = g[0, z + 1], g[1, z + 1]
        if level == 0:
            gws, ges = field_near(ADJ, 0, z, w), field_near(ADJ, 1, z, e)
        else:
            gws, ges = ([gnear[4 * f + d, z] for d in range(4)] for f in range(2))
        pu = pt = q1 = q2 = q3 = q4 = 0.0
        for zn in (z, z + 2):
            du, dt = m[0, zn] - u, m[1, zn] - t
            dw, de = g[0, zn] - w, g[1, zn] - e
            sp, hp = s + m[2, zn], h + m[3, zn]
            pu += sp * (c0 * dw + c3 * de)
            pt += hp * (c1 * dw + c2 * de)
            q1, q2, q3, q4 = q1 + du * dw, q2 + du * de, q3 + dt * dw, q4 + dt * de
        for d in range(4):
            sn = ss[d]
            hn = 0.75 + 0.5 * sn
            du, dt = us[d] - u, ts[d] - t
            dw, de = gws[d] - w, ges[d] - e
            pu += (kw + coef[1 + d, 0] * sn) * dw + (kv + coef[1 + d, 3] * sn) * de
            pt += (dtv + coef[1 + d, 1] * hn) * dw + (lamb + coef[1 + d, 2] * hn) * de
            q1, q2, q3, q4 = q1 + du * dw, q2 + du * de, q3 + dt * dw, q4 + dt * de
        bend = s - 1.5
        slope = 1.0 - bend * bend
        pu -= slope * (c0 * q1 + c3 * q2 + 0.5 * (c1 * q3 + c2 * q4))
        return w + 0.5 * pu, e + 0.5 * pt

    def put_edges(e, ref, z, pair, carry):
        for f in range(2):
            ref[f, z + 1] = pair[f]
            edges_x(e, row_of(f, z), pair[f])
            carry = edges_y(carry, row_of(f, z), pair[f])
        return carry

    def work1(z):
        near = state_near(0, z)
        pair = forward(0, z, near)
        return near, pair, strength(pair[0])

    def put1(z, found, carry):
        near, pair, s = found
        keep_near(near0, z, near)
        m1[2, z + 1] = s
        m1[3, z + 1] = 0.75 + 0.5 * s
        return put_edges(ST1, m1, z, pair, carry)

    for half in range(2):
        arrived(ST0, half)
        ys[1, half, 0], ys[1, half, 1] = by_chunks(half * hz, hz, 4, work1, put1, blank)
        start(ST1, half)

    def work2(z):
        near = state_near(1, z)
        return near, backward(1, z, near)

    def put2(z, found, carry):
        near, pair = found
        keep_near(near1, z, near)
        return put_edges(ADJ, g1, z, pair, carry)

    for half in range(2):
        arrived(ST1, half)
        ys[2, half, 0], ys[2, half, 1] = by_chunks(half * hz, hz, 4, work2, put2, blank)
        start(ADJ, half)

    def put_out(ref):
        def put(z, pair, _):
            for f in range(2):
                ref[f * nz + z] = pair[f]
            return 0
        return put

    written = []

    def write(i, held, out, half):
        for f in range(2):
            part = pl.ds(f * nz + half * hz, hz)
            copy = pltpu.make_async_copy(held.at[part], out.at[part], osem.at[i, half, f])
            copy.start()
            written.append(copy)

    for half in range(2):
        by_chunks(
            half * hz, hz, 4, lambda z: forward(1, z, kept_near(near1, z)), put_out(held2), 0
        )
        write(0, held2, out2, half)
    for half in range(2):
        arrived(ADJ, half)
        by_chunks(
            half * hz, hz, 4, lambda z: backward(0, z, kept_near(near0, z)), put_out(helds), 0
        )
        write(1, helds, outs, half)

    for copies in sent:
        for c in copies:
            c.wait_send()
    each(COT, 0, lambda c: c.wait_send())
    for e in (ST0, ST1, ADJ):
        for half in range(2):
            each(e, half, lambda c: c.wait_send())
    for copy in written:
        copy.wait()


def hand_over(a, b, a_out, b_out, held, in_sems, out_sems):
    parts = in_sems.shape[1]
    size = a.shape[0] // parts
    pieces = [(i, j) for j in range(parts) for i in range(2)]
    reads = [
        pltpu.make_async_copy(
            (a, b)[i].at[pl.ds(j * size, size)], held.at[i, pl.ds(j * size, size)], in_sems.at[i, j]
        )
        for i, j in pieces
    ]
    writes = [
        pltpu.make_async_copy(
            held.at[i, pl.ds(j * size, size)], (a_out, b_out)[i].at[pl.ds(j * size, size)], out_sems.at[i, j]
        )
        for i, j in pieces
    ]
    for c in reads:
        c.start()
    for read, write in zip(reads, writes):
        read.wait()
        write.start()
    for c in writes:
        c.wait()


def on_device(n_gx, n_gy, stored_slab, block_scales, holder, soil_class, soil_table, cotangent):
    _, nz, cx, cy = stored_slab.shape
    layers = 2 * nz
    assert n_gy % 2 == 0 and layers + 4 <= cy
    f32 = jnp.float32
    slab = stored_slab.reshape(nz, 2 * cx, cy)
    factors = jnp.transpose(block_scales, (2, 3, 0, 1)).reshape(2, nz)
    cot = cotangent.reshape(layers, cx, cy)
    hbm = pl.BlockSpec(memory_space=pltpu.HBM)
    out = jax.ShapeDtypeStruct((layers, cx, cy), f32)
    dma = pltpu.SemaphoreType.DMA
    state2, adjoint0 = pl.pallas_call(
        functools.partial(window, n_gx, n_gy, nz),
        out_shape=(out, out),
        in_specs=[hbm] * 6,
        out_specs=(hbm, hbm),
        scratch_shapes=[
            pltpu.SMEM(holder.shape, jnp.int32),
            pltpu.SMEM(soil_table.shape[::-1], f32),
            pltpu.VMEM((cx, cy), jnp.int32),
            pltpu.VMEM((2, nz), jnp.bfloat16),
            pltpu.VMEM((cx, cy), f32),
            pltpu.VMEM((n_gy, nz, 2 * cx, cy), jnp.bfloat16),
            pltpu.VMEM((n_gy, cx, cy), f32),
            pltpu.VMEM((4, nz + 2, cx, cy), f32),
            pltpu.VMEM((4, nz + 2, cx, cy), f32),
            pltpu.VMEM((2, nz + 2, cx, cy), f32),
            pltpu.VMEM((2, nz + 2, cx, cy), f32),
            pltpu.VMEM((2, nz, cx, cy), f32),
            pltpu.VMEM((2, nz, cx, cy), f32),
            pltpu.VMEM((12, nz, cx, cy), f32),
            pltpu.VMEM((12, nz, cx, cy), f32),
            pltpu.VMEM((8, nz, cx, cy), f32),
            pltpu.VMEM((layers, cx, cy), f32),
            pltpu.VMEM((layers, cx, cy), f32),
            pltpu.VMEM((4, 2, layers + 4, 1, cy), f32),
            pltpu.VMEM((4, 2, layers + 4, 1, cy), f32),
            pltpu.VMEM((3, 2, 2, cx, cy), f32),
            pltpu.VMEM((3, 2, 2, cx, cy), f32),
            pltpu.VMEM((5, 4, cx, cy), f32),
            dma((3, n_gy - 1)),
            dma((3, n_gy - 1)),
            dma((7,)),
            dma((2, 2, 2)),
            dma((4, 2, 2)),
            dma((4, 2, 2)),
            dma((3, 2, 2)),
            dma((3, 2, 2)),
        ],
        compiler_params=pltpu.CompilerParams(
            collective_id=0, has_side_effects=True, vmem_limit_bytes=60 * 1024 * 1024
        ),
        name="window",
    )(holder, soil_table.T, slab, factors, soil_class, cot)
    state2, adjoint0 = pl.pallas_call(
        hand_over,
        out_shape=(out, out),
        in_specs=[hbm, hbm],
        out_specs=(hbm, hbm),
        scratch_shapes=[pltpu.VMEM((2, layers, cx, cy), f32), dma((2, 4)), dma((2, 4))],
        compiler_params=pltpu.CompilerParams(vmem_limit_bytes=60 * 1024 * 1024),
        name="hand_over",
    )(state2, adjoint0)
    shape = cotangent.shape
    return state2.reshape(shape), adjoint0.reshape(shape)


def solution(mesh):
    placed = (
        P(None, None, "gx", "gy"),
        P(None, None, "gx", "gy"),
        P(),
        P("gx", "gy"),
        P(),
        P(None, None, "gx", "gy"),
    )
    return jax.shard_map(
        functools.partial(on_device, mesh.shape["gx"], mesh.shape["gy"]),
        mesh=mesh,
        in_specs=placed,
        out_specs=(P(None, None, "gx", "gy"), P(None, None, "gx", "gy")),
        check_vma=False,
    )
```

```python
import functools

import jax
import jax.numpy as jnp
from jax import lax
from jax.experimental import pallas as pl
from jax.experimental.pallas import tpu as pltpu
from jax.sharding import PartitionSpec as P

MESH = pl.DeviceIdType.MESH
COT, ST0, ST1, ADJ = range(4)


def window(
    n_gx, n_gy, nz, holder_in, table_in, slab_in, scale, classes_in, cot, out2, outs,
    holder, table, classes, scales, spread, slots, sslots, m0, m1, g0, g1, left0, right0, near0, near1,
    gnear, held2, helds, xs, xr, ys, yr, coef,
    gsend, grecv, lsem, osem, xsend, xrecv, ysend, yrecv,
):
    gx, gy = lax.axis_index("gx"), lax.axis_index("gy")
    cx, cy = classes.shape
    chips, hz = n_gy // 2, nz // 2
    partner = gy + 1 - 2 * lax.rem(gy, 2)
    lane = lax.broadcasted_iota(jnp.int32, (cx, cy), 1)
    sub = lax.broadcasted_iota(jnp.int32, (cx, cy), 0)
    first_row, last_row = sub == 0, sub == cx - 1
    first_lane, last_lane = lane == 0, lane == cy - 1
    x_has = (gx > 0, gx < n_gx - 1)
    y_has = (gy > 0, gy < n_gy - 1)

    barrier = pltpu.get_barrier_semaphore()
    for k in range(1, n_gy):
        pl.semaphore_signal(barrier, inc=1, device_id=(gx, lax.rem(gy + k, n_gy)), device_id_type=MESH)
    for side, there in ((0, gx - 1), (1, gx + 1)):
        @pl.when(x_has[side])
        def _():
            pl.semaphore_signal(barrier, inc=1, device_id=(there, gy), device_id_type=MESH)

    small = [
        pltpu.make_async_copy(table_in, table, lsem.at[0]),
        pltpu.make_async_copy(classes_in, classes, lsem.at[1]),
        pltpu.make_async_copy(holder_in, holder, lsem.at[2]),
    ]
    own = [
        pltpu.make_async_copy(slab_in, slots.at[gy], lsem.at[3]),
    ]
    scaling = pltpu.make_async_copy(scale, scales, lsem.at[4])
    cots = [
        pltpu.make_async_copy(
            cot.at[pl.ds(f * nz, nz)], g0.at[f, pl.ds(1, nz)], lsem.at[5 + f]
        )
        for f in range(2)
    ]
    for copy in own + [scaling] + small + cots:
        copy.start()
    greeted = n_gy - 1 + jnp.where(gx > 0, 1, 0) + jnp.where(gx < n_gx - 1, 1, 0)
    pl.semaphore_wait(barrier, greeted)

    def block_copies(index, slot, there, field):
        part = pl.ds(field * hz, hz)
        src = slab_in.at[part] if slot is gy else slots.at[slot, part]
        pieces = [(src, slots.at[slot, part], field)]
        if field == 1:
            pieces.append((sslots.at[slot], sslots.at[slot], 2))
        return [
            pltpu.make_async_remote_copy(
                src_ref=src, dst_ref=dst, send_sem=gsend.at[i, index],
                recv_sem=grecv.at[i, index], device_id=(gx, there), device_id_type=MESH,
            )
            for src, dst, i in pieces
        ]

    direct = [
        [block_copies(k, gy, lax.rem(gy + 2 * k, n_gy), field) for k in range(1, chips)]
        for field in range(2)
    ]
    beside = [block_copies(0, gy, partner, field) for field in range(2)]
    for field in range(2):
        for copies in direct[field] + [beside[field]]:
            copies[0].start()
    spread[...] = jnp.zeros((cx, cy), jnp.float32)
    scaling.wait()
    spread[0:2, 0:nz] = scales[...].astype(jnp.float32)
    sslots[gy] = jnp.where(
        lane < nz,
        jnp.broadcast_to(spread[0:1], (cx, cy)),
        pltpu.roll(jnp.broadcast_to(spread[1:2], (cx, cy)), nz, 1),
    )
    for copies in direct[1] + [beside[1]]:
        copies[1].start()

    for side in range(2):
        @pl.when(jnp.logical_not(x_has[side]))
        def _():
            for e in range(4):
                xr[e, side] = jnp.zeros(xr.shape[2:], jnp.float32)

        @pl.when(jnp.logical_not(y_has[side]))
        def _():
            for e in range(3):
                for half in range(2):
                    yr[e, half, side] = jnp.zeros((cx, cy), jnp.float32)

    def row_of(f, z):
        return z + f * hz + lax.div(z, hz) * hz

    for ref in (m0, m1, g0, g1):
        for q in range(ref.shape[0]):
            ref[q, 0] = jnp.zeros((cx, cy), jnp.float32)
            ref[q, nz + 1] = jnp.zeros((cx, cy), jnp.float32)

    def to_lane(value, lane_from, lane_to):
        return pltpu.roll(value, lax.rem(lane_to - lane_from + cy, cy), 1)

    def edges_x(e, row, value):
        xs[e, 0, row] = value[0:1]
        xs[e, 1, row] = value[cx - 1 : cx]

    def edges_y(carry, slot, value):
        low, high = carry
        here = lane == slot
        return (
            jnp.where(here, to_lane(value, 0, slot), low),
            jnp.where(here, to_lane(value, cy - 1, slot), high),
        )

    blank = (jnp.zeros((cx, cy), jnp.float32),) * 2

    def by_chunks(first, layers, size, work, store, carry):
        def chunk(i, carry):
            zs = [first + i * size + j for j in range(size)]
            found = [work(z) for z in zs]
            for z, value in zip(zs, found):
                carry = store(z, value, carry)
            return carry

        assert layers % size == 0
        return lax.fori_loop(0, layers // size, chunk, carry)

    for copy in small:
        copy.wait()
    kind = classes[...]
    for k in range(4):
        value = jnp.zeros((cx, cy), jnp.float32)
        for c in range(table.shape[1]):
            value = jnp.where(kind == c, table[k, c], value)
        coef[0, k] = value
        edges_x(COT, 2 * nz + k, value)

    def put_cot(z, values, carry):
        for f in range(2):
            edges_x(COT, row_of(f, z), values[f])
            carry = edges_y(carry, row_of(f, z), values[f])
        return carry

    for copy in cots:
        copy.wait()
    carry = by_chunks(0, nz, 8, lambda z: [g0[f, z + 1] for f in range(2)], put_cot, blank)
    for k in range(4):
        carry = edges_y(carry, 2 * nz + k, coef[0, k])
    ys[0, 0, 0], ys[0, 0, 1] = carry

    def x_copy(e, half, side):
        there = gx - 1 if side == 0 else gx + 1
        part = pl.ds(0, 2 * nz + 4) if e == COT else pl.ds(half * nz, nz)
        return pltpu.make_async_remote_copy(
            src_ref=xs.at[e, side, part], dst_ref=xr.at[e, 1 - side, part],
            send_sem=xsend.at[e, half, side], recv_sem=xrecv.at[e, half, 1 - side],
            device_id=(there, gy), device_id_type=MESH,
        )

    y_of = {COT: 0, ST1: 1, ADJ: 2}

    def y_copy(e, half, side):
        there = gy - 1 if side == 0 else gy + 1
        i = y_of[e]
        return pltpu.make_async_remote_copy(
            src_ref=ys.at[i, half, side], dst_ref=yr.at[i, half, 1 - side],
            send_sem=ysend.at[i, half, side], recv_sem=yrecv.at[i, half, 1 - side],
            device_id=(gx, there), device_id_type=MESH,
        )

    def each(e, half, act, mirrored=False):
        for make, has in ((x_copy, x_has), (y_copy, y_has)):
            if make is y_copy and e not in y_of:
                continue
            for side in range(2):
                @pl.when(has[side])
                def _():
                    act(make(e, half, 1 - side if mirrored else side))

    def start(e, half):
        each(e, half, lambda c: c.start())

    def arrived(e, half):
        each(e, half, lambda c: c.wait_recv(), mirrored=True)

    start(COT, 0)
    sent = direct[0] + direct[1] + beside
    onward = [[], []]

    def pass_on(field):
        for k in range(1, chips):
            for c in direct[field][k - 1]:
                c.wait_recv()
            copies = block_copies(chips - 1 + k, lax.rem(gy - 2 * k + n_gy, n_gy), partner, field)
            for c in copies:
                c.start()
            onward[field].append(copies)

    for field in range(2):
        pass_on(field)

    arrived(COT, 0)

    def beside_x(value, low, high):
        return (
            jnp.where(first_row, low, pltpu.roll(value, 1, 0)),
            jnp.where(last_row, high, pltpu.roll(value, cx - 1, 0)),
        )

    def beside_y(value, low, high, slot):
        return (
            jnp.where(first_lane, to_lane(low, slot, 0), pltpu.roll(value, 1, 1)),
            jnp.where(last_lane, to_lane(high, slot, cy - 1), pltpu.roll(value, cy - 1, 1)),
        )

    for k in range(4):
        value = coef[0, k]
        row = 2 * nz + k
        near = beside_x(value, xr[COT, 0, row], xr[COT, 1, row]) + beside_y(
            value, yr[0, 0, 0], yr[0, 0, 1], row
        )
        for d in range(4):
            coef[1 + d, k] = near[d]

    def rows(e, row):
        return xr[e, 0, row], xr[e, 1, row]

    def field_near(e, f, z, value):
        row, i, half = row_of(f, z), y_of[e], 0 if e == COT else lax.div(z, hz)
        return beside_x(value, *rows(e, row)) + beside_y(value, yr[i, half, 0], yr[i, half, 1], row)

    def keep_cot_near(z):
        for f in range(2):
            found = field_near(COT, f, z, g0[f, z + 1])
            for d in range(4):
                gnear[4 * f + d, z] = found[d]

    by_chunks(0, nz, 4, keep_cot_near, lambda z, found, _: 0, 0)

    sent += onward[0] + onward[1]
    for copies in beside + onward[0] + onward[1]:
        for c in copies:
            c.wait_recv()
    for copy in own:
        copy.wait()

    def strength(u):
        return 1.5 + jnp.tanh(u)

    def pair_of(index, factor):
        here = holder[index]
        factors = sslots[here] * factor

        def pair(p):
            both = slots[here, p].astype(jnp.float32)
            found = []
            for j in range(2):
                by = jnp.broadcast_to(to_lane(factors, 2 * p + j, 0)[:, 0:1], (cx, cy))
                found.append(both[j * cx : (j + 1) * cx] * by)
            return found

        return pair

    def put_own(p, found, _):
        values, strengths = found
        for j in range(2):
            l = 2 * p + j
            f, z = lax.div(l, nz), lax.rem(l, nz)
            m0[f, z + 1] = values[j]
            edges_x(ST0, row_of(f, z), values[j])
            if strengths:
                m0[2, z + 1] = strengths[j]
                m0[3, z + 1] = 0.75 + 0.5 * strengths[j]
        return 0

    def own_of(f):
        pair = pair_of(gy, 1.0)

        def work(p):
            values = pair(p)
            return values, [strength(v) for v in values] if f == 0 else None

        return work

    quarter = hz // 2
    for half in range(2):
        for f in range(2):
            by_chunks(f * hz + half * quarter, quarter, 8, own_of(f), put_own, 0)
        start(ST0, half)

    before = pair_of(jnp.maximum(gy - 1, 0), jnp.where(gy > 0, 1.0, 0.0))
    after = pair_of(jnp.minimum(gy + 1, n_gy - 1), jnp.where(gy < n_gy - 1, 1.0, 0.0))

    def put_sides(p, values, _):
        for ref, pair in zip((left0, right0), values):
            for j in range(2):
                l = 2 * p + j
                ref[l // nz, lax.rem(l, nz)] = pair[j]
        return 0

    by_chunks(0, nz, 4, lambda p: (before(p), after(p)), put_sides, 0)

    def state_near(level, z):
        m, e = (m0, ST0) if level == 0 else (m1, ST1)
        found = []
        for q in range(2):
            value = m[q, z + 1]
            if level == 0:
                near = beside_x(value, *rows(e, row_of(q, z))) + (
                    pltpu.roll(jnp.where(last_lane, left0[q, z], value), 1, 1),
                    pltpu.roll(jnp.where(first_lane, right0[q, z], value), cy - 1, 1),
                )
            else:
                near = field_near(ST1, q, z, value)
            found.append(near)
        found.append([strength(u) for u in found[0]])
        return found

    def keep_near(ref, z, found):
        for q in range(3):
            for d in range(4):
                ref[4 * q + d, z] = found[q][d]

    def kept_near(ref, z):
        return [[ref[4 * q + d, z] for d in range(4)] for q in range(3)]

    def forward(level, z, near):
        m = m0 if level == 0 else m1
        us, ts, ss = near
        u, t, s, h = (m[q, z + 1] for q in range(4))
        c0, c1, c2, c3 = (coef[0, k] for k in range(4))
        kw, dtv, lamb, kv = c0 * s, c1 * h, c2 * h, c3 * s
        a = b = None
        for zn in (z, z + 2):
            x = (s + m[2, zn]) * (m[0, zn] - u)
            y = (h + m[3, zn]) * (m[1, zn] - t)
            a, b = (x, y) if a is None else (a + x, b + y)
        water, energy = c0 * a + c1 * b, c2 * b + c3 * a
        for d in range(4):
            sn = ss[d]
            hn = 0.75 + 0.5 * sn
            du, dt = us[d] - u, ts[d] - t
            water += (kw + coef[1 + d, 0] * sn) * du + (dtv + coef[1 + d, 1] * hn) * dt
            energy += (lamb + coef[1 + d, 2] * hn) * dt + (kv + coef[1 + d, 3] * sn) * du
        return u + 0.5 * water, t + 0.5 * energy

    def backward(level, z, near):
        m, g = (m0, g1) if level == 0 else (m1, g0)
        us, ts, ss = near
        u, t, s, h = (m[q, z + 1] for q in range(4))
        c0, c1, c2, c3 = (coef[0, k] for k in range(4))
        kw, dtv, lamb, kv = c0 * s, c1 * h, c2 * h, c3 * s
        w, e = g[0, z + 1], g[1, z + 1]
        if level == 0:
            gws, ges = field_near(ADJ, 0, z, w), field_near(ADJ, 1, z, e)
        else:
            gws, ges = ([gnear[4 * f + d, z] for d in range(4)] for f in range(2))
        pu = pt = q1 = q2 = q3 = q4 = 0.0
        for zn in (z, z + 2):
            du, dt = m[0, zn] - u, m[1, zn] - t
            dw, de = g[0, zn] - w, g[1, zn] - e
            sp, hp = s + m[2, zn], h + m[3, zn]
            pu += sp * (c0 * dw + c3 * de)
            pt += hp * (c1 * dw + c2 * de)
            q1, q2, q3, q4 = q1 + du * dw, q2 + du * de, q3 + dt * dw, q4 + dt * de
        for d in range(4):
            sn = ss[d]
            hn = 0.75 + 0.5 * sn
            du, dt = us[d] - u, ts[d] - t
            dw, de = gws[d] - w, ges[d] - e
            pu += (kw + coef[1 + d, 0] * sn) * dw + (kv + coef[1 + d, 3] * sn) * de
            pt += (dtv + coef[1 + d, 1] * hn) * dw + (lamb + coef[1 + d, 2] * hn) * de
            q1, q2, q3, q4 = q1 + du * dw, q2 + du * de, q3 + dt * dw, q4 + dt * de
        bend = s - 1.5
        slope = 1.0 - bend * bend
        pu -= slope * (c0 * q1 + c3 * q2 + 0.5 * (c1 * q3 + c2 * q4))
        return w + 0.5 * pu, e + 0.5 * pt

    def put_edges(e, ref, z, pair, carry):
        for f in range(2):
            ref[f, z + 1] = pair[f]
            edges_x(e, row_of(f, z), pair[f])
            carry = edges_y(carry, row_of(f, z), pair[f])
        return carry

    def work1(z):
        near = state_near(0, z)
        keep_near(near0, z, near)
        pair = forward(0, z, near)
        return pair, strength(pair[0])

    def put1(z, found, carry):
        pair, s = found
        m1[2, z + 1] = s
        m1[3, z + 1] = 0.75 + 0.5 * s
        return put_edges(ST1, m1, z, pair, carry)

    for half in range(2):
        arrived(ST0, half)
        ys[1, half, 0], ys[1, half, 1] = by_chunks(half * hz, hz, 4, work1, put1, blank)
        start(ST1, half)

    def work2(z):
        near = state_near(1, z)
        keep_near(near1, z, near)
        return backward(1, z, near)

    def put2(z, pair, carry):
        return put_edges(ADJ, g1, z, pair, carry)

    for half in range(2):
        arrived(ST1, half)
        ys[2, half, 0], ys[2, half, 1] = by_chunks(half * hz, hz, 4, work2, put2, blank)
        start(ADJ, half)

    def put_out(ref):
        def put(z, pair, _):
            for f in range(2):
                ref[f * nz + z] = pair[f]
            return 0
        return put

    written = []

    def write(i, held, out, half):
        for f in range(2):
            part = pl.ds(f * nz + half * hz, hz)
            copy = pltpu.make_async_copy(held.at[part], out.at[part], osem.at[i, half, f])
            copy.start()
            written.append(copy)

    for half in range(2):
        by_chunks(
            half * hz, hz, 4, lambda z: forward(1, z, kept_near(near1, z)), put_out(held2), 0
        )
        write(0, held2, out2, half)
    for half in range(2):
        arrived(ADJ, half)
        by_chunks(
            half * hz, hz, 4, lambda z: backward(0, z, kept_near(near0, z)), put_out(helds), 0
        )
        write(1, helds, outs, half)

    for copies in sent:
        for c in copies:
            c.wait_send()
    each(COT, 0, lambda c: c.wait_send())
    for e in (ST0, ST1, ADJ):
        for half in range(2):
            each(e, half, lambda c: c.wait_send())
    for copy in written:
        copy.wait()


def hand_over(a, b, a_out, b_out, held, in_sems, out_sems):
    parts = in_sems.shape[1]
    size = a.shape[0] // parts
    pieces = [(i, j) for j in range(parts) for i in range(2)]
    reads = [
        pltpu.make_async_copy(
            (a, b)[i].at[pl.ds(j * size, size)], held.at[i, pl.ds(j * size, size)], in_sems.at[i, j]
        )
        for i, j in pieces
    ]
    writes = [
        pltpu.make_async_copy(
            held.at[i, pl.ds(j * size, size)], (a_out, b_out)[i].at[pl.ds(j * size, size)], out_sems.at[i, j]
        )
        for i, j in pieces
    ]
    for c in reads:
        c.start()
    for read, write in zip(reads, writes):
        read.wait()
        write.start()
    for c in writes:
        c.wait()


def on_device(n_gx, n_gy, stored_slab, block_scales, holder, soil_class, soil_table, cotangent):
    _, nz, cx, cy = stored_slab.shape
    layers = 2 * nz
    assert n_gy % 2 == 0 and layers + 4 <= cy
    f32 = jnp.float32
    slab = stored_slab.reshape(nz, 2 * cx, cy)
    factors = jnp.transpose(block_scales, (2, 3, 0, 1)).reshape(2, nz)
    cot = cotangent.reshape(layers, cx, cy)
    hbm = pl.BlockSpec(memory_space=pltpu.HBM)
    out = jax.ShapeDtypeStruct((layers, cx, cy), f32)
    dma = pltpu.SemaphoreType.DMA
    state2, adjoint0 = pl.pallas_call(
        functools.partial(window, n_gx, n_gy, nz),
        out_shape=(out, out),
        in_specs=[hbm] * 6,
        out_specs=(hbm, hbm),
        scratch_shapes=[
            pltpu.SMEM(holder.shape, jnp.int32),
            pltpu.SMEM(soil_table.shape[::-1], f32),
            pltpu.VMEM((cx, cy), jnp.int32),
            pltpu.VMEM((2, nz), jnp.bfloat16),
            pltpu.VMEM((cx, cy), f32),
            pltpu.VMEM((n_gy, nz, 2 * cx, cy), jnp.bfloat16),
            pltpu.VMEM((n_gy, cx, cy), f32),
            pltpu.VMEM((4, nz + 2, cx, cy), f32),
            pltpu.VMEM((4, nz + 2, cx, cy), f32),
            pltpu.VMEM((2, nz + 2, cx, cy), f32),
            pltpu.VMEM((2, nz + 2, cx, cy), f32),
            pltpu.VMEM((2, nz, cx, cy), f32),
            pltpu.VMEM((2, nz, cx, cy), f32),
            pltpu.VMEM((12, nz, cx, cy), f32),
            pltpu.VMEM((12, nz, cx, cy), f32),
            pltpu.VMEM((8, nz, cx, cy), f32),
            pltpu.VMEM((layers, cx, cy), f32),
            pltpu.VMEM((layers, cx, cy), f32),
            pltpu.VMEM((4, 2, layers + 4, 1, cy), f32),
            pltpu.VMEM((4, 2, layers + 4, 1, cy), f32),
            pltpu.VMEM((3, 2, 2, cx, cy), f32),
            pltpu.VMEM((3, 2, 2, cx, cy), f32),
            pltpu.VMEM((5, 4, cx, cy), f32),
            dma((3, n_gy - 1)),
            dma((3, n_gy - 1)),
            dma((7,)),
            dma((2, 2, 2)),
            dma((4, 2, 2)),
            dma((4, 2, 2)),
            dma((3, 2, 2)),
            dma((3, 2, 2)),
        ],
        compiler_params=pltpu.CompilerParams(
            collective_id=0, has_side_effects=True, vmem_limit_bytes=60 * 1024 * 1024
        ),
        name="window",
    )(holder, soil_table.T, slab, factors, soil_class, cot)
    state2, adjoint0 = pl.pallas_call(
        hand_over,
        out_shape=(out, out),
        in_specs=[hbm, hbm],
        out_specs=(hbm, hbm),
        scratch_shapes=[pltpu.VMEM((2, layers, cx, cy), f32), dma((2, 4)), dma((2, 4))],
        compiler_params=pltpu.CompilerParams(vmem_limit_bytes=60 * 1024 * 1024),
        name="hand_over",
    )(state2, adjoint0)
    shape = cotangent.shape
    return state2.reshape(shape), adjoint0.reshape(shape)


def solution(mesh):
    placed = (
        P(None, None, "gx", "gy"),
        P(None, None, "gx", "gy"),
        P(),
        P("gx", "gy"),
        P(),
        P(None, None, "gx", "gy"),
    )
    return jax.shard_map(
        functools.partial(on_device, mesh.shape["gx"], mesh.shape["gy"]),
        mesh=mesh,
        in_specs=placed,
        out_specs=(P(None, None, "gx", "gy"), P(None, None, "gx", "gy")),
        check_vma=False,
    )
```

```python
import functools

import jax
import jax.numpy as jnp
from jax import lax
from jax.experimental import pallas as pl
from jax.experimental.pallas import tpu as pltpu
from jax.sharding import PartitionSpec as P

MESH = pl.DeviceIdType.MESH
COT, ST0, ST1, ADJ = range(4)
PARTS = 4


def window(
    n_gx, n_gy, nz, holder_in, table_in, slab_in, scale, classes_in, cot, out2, outs,
    holder, table, classes, scales, spread, slots, sslots, m0, m1, g0, g1, left0, right0, near0, near1,
    gnear, held2, helds, xs, xr, ys, yr, coef,
    gsend, grecv, lsem, osem, xsend, xrecv, ysend, yrecv,
):
    gx, gy = lax.axis_index("gx"), lax.axis_index("gy")
    cx, cy = classes.shape
    chips, hz, qz = n_gy // 2, nz // 2, nz // PARTS
    partner = gy + 1 - 2 * lax.rem(gy, 2)
    lane = lax.broadcasted_iota(jnp.int32, (cx, cy), 1)
    sub = lax.broadcasted_iota(jnp.int32, (cx, cy), 0)
    first_row, last_row = sub == 0, sub == cx - 1
    first_lane, last_lane = lane == 0, lane == cy - 1
    x_has = (gx > 0, gx < n_gx - 1)
    y_has = (gy > 0, gy < n_gy - 1)

    barrier = pltpu.get_barrier_semaphore()
    for k in range(1, n_gy):
        pl.semaphore_signal(barrier, inc=1, device_id=(gx, lax.rem(gy + k, n_gy)), device_id_type=MESH)
    for side, there in ((0, gx - 1), (1, gx + 1)):
        @pl.when(x_has[side])
        def _():
            pl.semaphore_signal(barrier, inc=1, device_id=(there, gy), device_id_type=MESH)

    small = [
        pltpu.make_async_copy(table_in, table, lsem.at[0]),
        pltpu.make_async_copy(classes_in, classes, lsem.at[1]),
        pltpu.make_async_copy(holder_in, holder, lsem.at[2]),
    ]
    own = [
        pltpu.make_async_copy(slab_in, slots.at[gy], lsem.at[3]),
    ]
    scaling = pltpu.make_async_copy(scale, scales, lsem.at[4])
    cots = [
        pltpu.make_async_copy(
            cot.at[pl.ds(f * nz, nz)], g0.at[f, pl.ds(1, nz)], lsem.at[5 + f]
        )
        for f in range(2)
    ]
    for copy in own + [scaling] + small + cots:
        copy.start()
    greeted = n_gy - 1 + jnp.where(gx > 0, 1, 0) + jnp.where(gx < n_gx - 1, 1, 0)
    pl.semaphore_wait(barrier, greeted)

    def block_copies(index, slot, there, field):
        part = pl.ds(field * hz, hz)
        src = slab_in.at[part] if slot is gy else slots.at[slot, part]
        pieces = [(src, slots.at[slot, part], field)]
        if field == 1:
            pieces.append((sslots.at[slot], sslots.at[slot], 2))
        return [
            pltpu.make_async_remote_copy(
                src_ref=src, dst_ref=dst, send_sem=gsend.at[i, index],
                recv_sem=grecv.at[i, index], device_id=(gx, there), device_id_type=MESH,
            )
            for src, dst, i in pieces
        ]

    direct = [
        [block_copies(k, gy, lax.rem(gy + 2 * k, n_gy), field) for k in range(1, chips)]
        for field in range(2)
    ]
    beside = [block_copies(0, gy, partner, field) for field in range(2)]
    for field in range(2):
        for copies in direct[field] + [beside[field]]:
            copies[0].start()
    spread[...] = jnp.zeros((cx, cy), jnp.float32)
    scaling.wait()
    spread[0:2, 0:nz] = scales[...].astype(jnp.float32)
    sslots[gy] = jnp.where(
        lane < nz,
        jnp.broadcast_to(spread[0:1], (cx, cy)),
        pltpu.roll(jnp.broadcast_to(spread[1:2], (cx, cy)), nz, 1),
    )
    for copies in direct[1] + [beside[1]]:
        copies[1].start()

    for side in range(2):
        @pl.when(jnp.logical_not(x_has[side]))
        def _():
            for e in range(4):
                xr[e, side] = jnp.zeros(xr.shape[2:], jnp.float32)

        @pl.when(jnp.logical_not(y_has[side]))
        def _():
            for e in range(3):
                for half in range(PARTS):
                    yr[e, half, side] = jnp.zeros((cx, cy), jnp.float32)

    def row_of(f, z):
        return z + (f + lax.div(z, qz)) * qz

    for ref in (m0, m1, g0, g1):
        for q in range(ref.shape[0]):
            ref[q, 0] = jnp.zeros((cx, cy), jnp.float32)
            ref[q, nz + 1] = jnp.zeros((cx, cy), jnp.float32)

    def to_lane(value, lane_from, lane_to):
        return pltpu.roll(value, lax.rem(lane_to - lane_from + cy, cy), 1)

    def edges_x(e, row, value):
        xs[e, 0, row] = value[0:1]
        xs[e, 1, row] = value[cx - 1 : cx]

    def edges_y(carry, slot, value):
        low, high = carry
        here = lane == slot
        return (
            jnp.where(here, to_lane(value, 0, slot), low),
            jnp.where(here, to_lane(value, cy - 1, slot), high),
        )

    blank = (jnp.zeros((cx, cy), jnp.float32),) * 2

    def by_chunks(first, layers, size, work, store, carry):
        def chunk(i, carry):
            zs = [first + i * size + j for j in range(size)]
            found = [work(z) for z in zs]
            for z, value in zip(zs, found):
                carry = store(z, value, carry)
            return carry

        assert layers % size == 0
        return lax.fori_loop(0, layers // size, chunk, carry)

    for copy in small:
        copy.wait()
    kind = classes[...]
    for k in range(4):
        value = jnp.zeros((cx, cy), jnp.float32)
        for c in range(table.shape[1]):
            value = jnp.where(kind == c, table[k, c], value)
        coef[0, k] = value
        edges_x(COT, 2 * nz + k, value)

    def put_cot(z, values, carry):
        for f in range(2):
            edges_x(COT, row_of(f, z), values[f])
            carry = edges_y(carry, row_of(f, z), values[f])
        return carry

    for copy in cots:
        copy.wait()
    carry = by_chunks(0, nz, 8, lambda z: [g0[f, z + 1] for f in range(2)], put_cot, blank)
    for k in range(4):
        carry = edges_y(carry, 2 * nz + k, coef[0, k])
    ys[0, 0, 0], ys[0, 0, 1] = carry

    def x_copy(e, half, side):
        there = gx - 1 if side == 0 else gx + 1
        part = pl.ds(0, 2 * nz + 4) if e == COT else pl.ds(half * 2 * qz, 2 * qz)
        return pltpu.make_async_remote_copy(
            src_ref=xs.at[e, side, part], dst_ref=xr.at[e, 1 - side, part],
            send_sem=xsend.at[e, half, side], recv_sem=xrecv.at[e, half, 1 - side],
            device_id=(there, gy), device_id_type=MESH,
        )

    y_of = {COT: 0, ST1: 1, ADJ: 2}

    def y_copy(e, half, side):
        there = gy - 1 if side == 0 else gy + 1
        i = y_of[e]
        return pltpu.make_async_remote_copy(
            src_ref=ys.at[i, half, side], dst_ref=yr.at[i, half, 1 - side],
            send_sem=ysend.at[i, half, side], recv_sem=yrecv.at[i, half, 1 - side],
            device_id=(gx, there), device_id_type=MESH,
        )

    def each(e, half, act, mirrored=False):
        for make, has in ((x_copy, x_has), (y_copy, y_has)):
            if make is y_copy and e not in y_of:
                continue
            for side in range(2):
                @pl.when(has[side])
                def _():
                    act(make(e, half, 1 - side if mirrored else side))

    def start(e, half):
        each(e, half, lambda c: c.start())

    def arrived(e, half):
        each(e, half, lambda c: c.wait_recv(), mirrored=True)

    start(COT, 0)
    sent = direct[0] + direct[1] + beside
    onward = [[], []]

    def pass_on(field):
        for k in range(1, chips):
            for c in direct[field][k - 1]:
                c.wait_recv()
            copies = block_copies(chips - 1 + k, lax.rem(gy - 2 * k + n_gy, n_gy), partner, field)
            for c in copies:
                c.start()
            onward[field].append(copies)

    for field in range(2):
        pass_on(field)

    arrived(COT, 0)

    def beside_x(value, low, high):
        return (
            jnp.where(first_row, low, pltpu.roll(value, 1, 0)),
            jnp.where(last_row, high, pltpu.roll(value, cx - 1, 0)),
        )

    def beside_y(value, low, high, slot):
        return (
            jnp.where(first_lane, to_lane(low, slot, 0), pltpu.roll(value, 1, 1)),
            jnp.where(last_lane, to_lane(high, slot, cy - 1), pltpu.roll(value, cy - 1, 1)),
        )

    for k in range(4):
        value = coef[0, k]
        row = 2 * nz + k
        near = beside_x(value, xr[COT, 0, row], xr[COT, 1, row]) + beside_y(
            value, yr[0, 0, 0], yr[0, 0, 1], row
        )
        for d in range(4):
            coef[1 + d, k] = near[d]

    def rows(e, row):
        return xr[e, 0, row], xr[e, 1, row]

    def field_near(e, f, z, value):
        row, i, half = row_of(f, z), y_of[e], 0 if e == COT else lax.div(z, qz)
        return beside_x(value, *rows(e, row)) + beside_y(value, yr[i, half, 0], yr[i, half, 1], row)

    def keep_cot_near(z):
        for f in range(2):
            found = field_near(COT, f, z, g0[f, z + 1])
            for d in range(4):
                gnear[4 * f + d, z] = found[d]

    by_chunks(0, nz, 4, keep_cot_near, lambda z, found, _: 0, 0)

    sent += onward[0] + onward[1]
    for copies in beside + onward[0] + onward[1]:
        for c in copies:
            c.wait_recv()
    for copy in own:
        copy.wait()

    def strength(u):
        return 1.5 + jnp.tanh(u)

    def pair_of(index, factor):
        here = holder[index]
        factors = sslots[here] * factor

        def pair(p):
            both = slots[here, p].astype(jnp.float32)
            found = []
            for j in range(2):
                by = jnp.broadcast_to(to_lane(factors, 2 * p + j, 0)[:, 0:1], (cx, cy))
                found.append(both[j * cx : (j + 1) * cx] * by)
            return found

        return pair

    def put_own(p, found, _):
        values, strengths = found
        for j in range(2):
            l = 2 * p + j
            f, z = lax.div(l, nz), lax.rem(l, nz)
            m0[f, z + 1] = values[j]
            edges_x(ST0, row_of(f, z), values[j])
            if strengths:
                m0[2, z + 1] = strengths[j]
                m0[3, z + 1] = 0.75 + 0.5 * strengths[j]
        return 0

    def own_of(f):
        pair = pair_of(gy, 1.0)

        def work(p):
            values = pair(p)
            return values, [strength(v) for v in values] if f == 0 else None

        return work

    quarter = qz // 2
    for half in range(PARTS):
        for f in range(2):
            by_chunks(f * hz + half * quarter, quarter, 4, own_of(f), put_own, 0)
        start(ST0, half)

    before = pair_of(jnp.maximum(gy - 1, 0), jnp.where(gy > 0, 1.0, 0.0))
    after = pair_of(jnp.minimum(gy + 1, n_gy - 1), jnp.where(gy < n_gy - 1, 1.0, 0.0))

    def put_sides(p, values, _):
        for ref, pair in zip((left0, right0), values):
            for j in range(2):
                l = 2 * p + j
                ref[l // nz, lax.rem(l, nz)] = pair[j]
        return 0

    by_chunks(0, nz, 4, lambda p: (before(p), after(p)), put_sides, 0)

    def state_near(level, z):
        m, e = (m0, ST0) if level == 0 else (m1, ST1)
        found = []
        for q in range(2):
            value = m[q, z + 1]
            if level == 0:
                near = beside_x(value, *rows(e, row_of(q, z))) + (
                    pltpu.roll(jnp.where(last_lane, left0[q, z], value), 1, 1),
                    pltpu.roll(jnp.where(first_lane, right0[q, z], value), cy - 1, 1),
                )
            else:
                near = field_near(ST1, q, z, value)
            found.append(near)
        found.append([strength(u) for u in found[0]])
        return found

    def keep_near(ref, z, found):
        for q in range(3):
            for d in range(4):
                ref[4 * q + d, z] = found[q][d]

    def kept_near(ref, z):
        return [[ref[4 * q + d, z] for d in range(4)] for q in range(3)]

    def forward(level, z, near):
        m = m0 if level == 0 else m1
        us, ts, ss = near
        u, t, s, h = (m[q, z + 1] for q in range(4))
        c0, c1, c2, c3 = (coef[0, k] for k in range(4))
        kw, dtv, lamb, kv = c0 * s, c1 * h, c2 * h, c3 * s
        a = b = None
        for zn in (z, z + 2):
            x = (s + m[2, zn]) * (m[0, zn] - u)
            y = (h + m[3, zn]) * (m[1, zn] - t)
            a, b = (x, y) if a is None else (a + x, b + y)
        water, energy = c0 * a + c1 * b, c2 * b + c3 * a
        for d in range(4):
            sn = ss[d]
            hn = 0.75 + 0.5 * sn
            du, dt = us[d] - u, ts[d] - t
            water += (kw + coef[1 + d, 0] * sn) * du + (dtv + coef[1 + d, 1] * hn) * dt
            energy += (lamb + coef[1 + d, 2] * hn) * dt + (kv + coef[1 + d, 3] * sn) * du
        return u + 0.5 * water, t + 0.5 * energy

    def backward(level, z, near):
        m, g = (m0, g1) if level == 0 else (m1, g0)
        us, ts, ss = near
        u, t, s, h = (m[q, z + 1] for q in range(4))
        c0, c1, c2, c3 = (coef[0, k] for k in range(4))
        kw, dtv, lamb, kv = c0 * s, c1 * h, c2 * h, c3 * s
        w, e = g[0, z + 1], g[1, z + 1]
        if level == 0:
            gws, ges = field_near(ADJ, 0, z, w), field_near(ADJ, 1, z, e)
        else:
            gws, ges = ([gnear[4 * f + d, z] for d in range(4)] for f in range(2))
        pu = pt = q1 = q2 = q3 = q4 = 0.0
        for zn in (z, z + 2):
            du, dt = m[0, zn] - u, m[1, zn] - t
            dw, de = g[0, zn] - w, g[1, zn] - e
            sp, hp = s + m[2, zn], h + m[3, zn]
            pu += sp * (c0 * dw + c3 * de)
            pt += hp * (c1 * dw + c2 * de)
            q1, q2, q3, q4 = q1 + du * dw, q2 + du * de, q3 + dt * dw, q4 + dt * de
        for d in range(4):
            sn = ss[d]
            hn = 0.75 + 0.5 * sn
            du, dt = us[d] - u, ts[d] - t
            dw, de = gws[d] - w, ges[d] - e
            pu += (kw + coef[1 + d, 0] * sn) * dw + (kv + coef[1 + d, 3] * sn) * de
            pt += (dtv + coef[1 + d, 1] * hn) * dw + (lamb + coef[1 + d, 2] * hn) * de
            q1, q2, q3, q4 = q1 + du * dw, q2 + du * de, q3 + dt * dw, q4 + dt * de
        bend = s - 1.5
        slope = 1.0 - bend * bend
        pu -= slope * (c0 * q1 + c3 * q2 + 0.5 * (c1 * q3 + c2 * q4))
        return w + 0.5 * pu, e + 0.5 * pt

    def put_edges(e, ref, z, pair, carry):
        for f in range(2):
            ref[f, z + 1] = pair[f]
            edges_x(e, row_of(f, z), pair[f])
            carry = edges_y(carry, row_of(f, z), pair[f])
        return carry

    def work1(z):
        near = state_near(0, z)
        keep_near(near0, z, near)
        pair = forward(0, z, near)
        return pair, strength(pair[0])

    def put1(z, found, carry):
        pair, s = found
        m1[2, z + 1] = s
        m1[3, z + 1] = 0.75 + 0.5 * s
        return put_edges(ST1, m1, z, pair, carry)

    for half in range(PARTS):
        arrived(ST0, half)
        ys[1, half, 0], ys[1, half, 1] = by_chunks(half * qz, qz, 4, work1, put1, blank)
        start(ST1, half)

    def work2(z):
        near = state_near(1, z)
        keep_near(near1, z, near)
        return backward(1, z, near)

    def put2(z, pair, carry):
        return put_edges(ADJ, g1, z, pair, carry)

    for half in range(PARTS):
        arrived(ST1, half)
        ys[2, half, 0], ys[2, half, 1] = by_chunks(half * qz, qz, 4, work2, put2, blank)
        start(ADJ, half)

    def put_out(ref):
        def put(z, pair, _):
            for f in range(2):
                ref[f * nz + z] = pair[f]
            return 0
        return put

    written = []

    def write(i, held, out, half):
        for f in range(2):
            part = pl.ds(f * nz + half * qz, qz)
            copy = pltpu.make_async_copy(held.at[part], out.at[part], osem.at[i, half, f])
            copy.start()
            written.append(copy)

    for half in range(PARTS):
        by_chunks(
            half * qz, qz, 4, lambda z: forward(1, z, kept_near(near1, z)), put_out(held2), 0
        )
        write(0, held2, out2, half)
    for half in range(PARTS):
        arrived(ADJ, half)
        by_chunks(
            half * qz, qz, 4, lambda z: backward(0, z, kept_near(near0, z)), put_out(helds), 0
        )
        write(1, helds, outs, half)

    for copies in sent:
        for c in copies:
            c.wait_send()
    each(COT, 0, lambda c: c.wait_send())
    for e in (ST0, ST1, ADJ):
        for half in range(PARTS):
            each(e, half, lambda c: c.wait_send())
    for copy in written:
        copy.wait()


def hand_over(a, b, a_out, b_out, held, in_sems, out_sems):
    parts = in_sems.shape[1]
    size = a.shape[0] // parts
    pieces = [(i, j) for j in range(parts) for i in range(2)]
    reads = [
        pltpu.make_async_copy(
            (a, b)[i].at[pl.ds(j * size, size)], held.at[i, pl.ds(j * size, size)], in_sems.at[i, j]
        )
        for i, j in pieces
    ]
    writes = [
        pltpu.make_async_copy(
            held.at[i, pl.ds(j * size, size)], (a_out, b_out)[i].at[pl.ds(j * size, size)], out_sems.at[i, j]
        )
        for i, j in pieces
    ]
    for c in reads:
        c.start()
    for read, write in zip(reads, writes):
        read.wait()
        write.start()
    for c in writes:
        c.wait()


def on_device(n_gx, n_gy, stored_slab, block_scales, holder, soil_class, soil_table, cotangent):
    _, nz, cx, cy = stored_slab.shape
    layers = 2 * nz
    assert n_gy % 2 == 0 and layers + 4 <= cy
    f32 = jnp.float32
    slab = stored_slab.reshape(nz, 2 * cx, cy)
    factors = jnp.transpose(block_scales, (2, 3, 0, 1)).reshape(2, nz)
    cot = cotangent.reshape(layers, cx, cy)
    hbm = pl.BlockSpec(memory_space=pltpu.HBM)
    out = jax.ShapeDtypeStruct((layers, cx, cy), f32)
    dma = pltpu.SemaphoreType.DMA
    state2, adjoint0 = pl.pallas_call(
        functools.partial(window, n_gx, n_gy, nz),
        out_shape=(out, out),
        in_specs=[hbm] * 6,
        out_specs=(hbm, hbm),
        scratch_shapes=[
            pltpu.SMEM(holder.shape, jnp.int32),
            pltpu.SMEM(soil_table.shape[::-1], f32),
            pltpu.VMEM((cx, cy), jnp.int32),
            pltpu.VMEM((2, nz), jnp.bfloat16),
            pltpu.VMEM((cx, cy), f32),
            pltpu.VMEM((n_gy, nz, 2 * cx, cy), jnp.bfloat16),
            pltpu.VMEM((n_gy, cx, cy), f32),
            pltpu.VMEM((4, nz + 2, cx, cy), f32),
            pltpu.VMEM((4, nz + 2, cx, cy), f32),
            pltpu.VMEM((2, nz + 2, cx, cy), f32),
            pltpu.VMEM((2, nz + 2, cx, cy), f32),
            pltpu.VMEM((2, nz, cx, cy), f32),
            pltpu.VMEM((2, nz, cx, cy), f32),
            pltpu.VMEM((12, nz, cx, cy), f32),
            pltpu.VMEM((12, nz, cx, cy), f32),
            pltpu.VMEM((8, nz, cx, cy), f32),
            pltpu.VMEM((layers, cx, cy), f32),
            pltpu.VMEM((layers, cx, cy), f32),
            pltpu.VMEM((4, 2, layers + 4, 1, cy), f32),
            pltpu.VMEM((4, 2, layers + 4, 1, cy), f32),
            pltpu.VMEM((3, PARTS, 2, cx, cy), f32),
            pltpu.VMEM((3, PARTS, 2, cx, cy), f32),
            pltpu.VMEM((5, 4, cx, cy), f32),
            dma((3, n_gy - 1)),
            dma((3, n_gy - 1)),
            dma((7,)),
            dma((2, PARTS, 2)),
            dma((4, PARTS, 2)),
            dma((4, PARTS, 2)),
            dma((3, PARTS, 2)),
            dma((3, PARTS, 2)),
        ],
        compiler_params=pltpu.CompilerParams(
            collective_id=0, has_side_effects=True, vmem_limit_bytes=60 * 1024 * 1024
        ),
        name="window",
    )(holder, soil_table.T, slab, factors, soil_class, cot)
    state2, adjoint0 = pl.pallas_call(
        hand_over,
        out_shape=(out, out),
        in_specs=[hbm, hbm],
        out_specs=(hbm, hbm),
        scratch_shapes=[pltpu.VMEM((2, layers, cx, cy), f32), dma((2, 4)), dma((2, 4))],
        compiler_params=pltpu.CompilerParams(vmem_limit_bytes=60 * 1024 * 1024),
        name="hand_over",
    )(state2, adjoint0)
    shape = cotangent.shape
    return state2.reshape(shape), adjoint0.reshape(shape)


def solution(mesh):
    placed = (
        P(None, None, "gx", "gy"),
        P(None, None, "gx", "gy"),
        P(),
        P("gx", "gy"),
        P(),
        P(None, None, "gx", "gy"),
    )
    return jax.shard_map(
        functools.partial(on_device, mesh.shape["gx"], mesh.shape["gy"]),
        mesh=mesh,
        in_specs=placed,
        out_specs=(P(None, None, "gx", "gy"), P(None, None, "gx", "gy")),
        check_vma=False,
    )
```
